512 devices in a mesh: ens: 32 (over z, x_lo), grid: 16 (over y, x_hi, core).
Axes of the slice: x: 4 (x_hi: 2, x_lo: 2; x = x_hi * 2 + x_lo), y: 4, z: 16, core: 2. Of those that a mesh axis runs over, the one named last changes fastest.
Arguments:
- hidden: bfloat16 [32, 12288, 1024], P('ens', 'grid'), may hold values from -6 to 6
- weight: bfloat16 [100, 1024], replicated, may hold values from -0.1875 to 0.1875
- bias: float32 [100], replicated, may hold values from -3 to 3
- target: float32 [100, 12288], P(None, 'grid'), may hold values from -6 to 6
- area_weight: float32 [12288], P('grid'), may hold values from 0.3 to 3
- var_weight: float32 [100], replicated, may hold values from 0.3 to 3
Outputs:
- loss: float32 [], replicated
- grad_hidden: bfloat16 [32, 12288, 1024], P('ens', 'grid')
- grad_weight: float32 [100, 1024], replicated
- grad_bias: float32 [100], replicated
The draws below stay inside these ranges and needn't reach their ends.
All inputs are finite; a program needn't handle non-finite values.
Results may differ from the reference program's by a relative error of at most 0.013.
Values may be sent and summed in bfloat16 or wider, within the bound.
A program may use at most 64 MiB of HBM per device.

```python
import math
import jax
import jax.numpy as jnp
from jax import lax

V = 100
H = 1024
MEMBERS = 32
GRID_PTS = 12288


def block_scale(rng, dims, cuts, smallest, largest):
    def one(position, shards_of):
        heights = jax.random.uniform(jax.random.fold_in(jax.random.fold_in(rng, 6), position), (shards_of,), jnp.float32, smallest / len(cuts), largest / len(cuts))
        return jnp.repeat(jnp.exp(heights), dims[position] // shards_of).reshape((-1,) + (1,) * (len(dims) - position - 1))

    loudness = one(*cuts[0])
    for cut in cuts[1:]:
        loudness = loudness * one(*cut)
    return loudness


def centred(own_key, dims, scale, reach, shards=(), held_as=jnp.bfloat16):
    result = jax.random.normal(own_key, dims, jnp.float32) * scale
    if len(shards) > 0:
        result = block_scale(own_key, dims, shards, -0.22, 0.18) * result
    return jnp.clip(result, min=-reach, max=reach).astype(held_as)


def setup_inputs(seed: int = 0) -> dict:
    splits = jax.random.split(jax.random.key(seed), 7)
    return {
        "hidden": centred(splits[0], (MEMBERS, GRID_PTS, H), 1.0, 6.0, ((0, 32), (1, 16))),
        "weight": centred(splits[1], (V, H), H ** -0.5, 0.1875),
        "bias": centred(splits[2], (V,), 0.5, 3.0, (), jnp.float32),
        "target": centred(splits[3], (V, GRID_PTS), 1.0, 6.0, ((1, 16),), jnp.float32),
        "area_weight": jnp.clip(jnp.exp(math.log(3.0) - 2.3025851 * jax.random.uniform(splits[4], (GRID_PTS,), jnp.float32) ** block_scale(splits[4], (GRID_PTS,), ((0, 16),), -0.2, 0.2)), 0.3, 3.0),
        "var_weight": jnp.clip(jnp.exp(jax.random.uniform(splits[5], (V,), jnp.float32, math.log(0.3), math.log(3.0))), 0.3, 3.0),
    }


alpha_fair = 0.95
smooth = 0.3

def soft_abs(diff):
    return jnp.sqrt(diff * diff + smooth * smooth) - smooth

def soft_sign(diff):
    return diff / jnp.sqrt(diff * diff + smooth * smooth)

def reference(hidden, weight, bias, target, area_weight, var_weight):
    members = hidden.shape[0]
    points = hidden.shape[1]
    width_v = weight.shape[0]

    def project(rows):
        return jnp.dot(weight, rows.T, preferred_element_type=jnp.float32)
    raw = lax.map(project, hidden)
    pred = (raw + bias[None, :, None]).astype(jnp.bfloat16)
    values = pred.astype(jnp.float32)

    def partner(carry, other):
        diff = values - other[None]
        return ((carry[0] + soft_sign(diff), carry[1] + soft_abs(diff)), None)
    zeros = jnp.zeros(values.shape, jnp.float32)
    (pair_sign, pair_abs), _ = lax.scan(partner, (zeros, zeros), values)
    eps = (1.0 - alpha_fair) / members
    crps = lax.optimization_barrier(jnp.sum(soft_abs(values - target[None]), axis=0)) / members
    crps = crps - (1.0 - eps) / (2.0 * members * (members - 1)) * lax.optimization_barrier(jnp.sum(pair_abs, axis=0))
    scale = var_weight[:, None] * area_weight[None, :]
    loss = jnp.sum(scale * crps) / (points * width_v)
    pair_coef = (1.0 - eps) / (members - 1)
    grad_pred = (scale[None] * (soft_sign(values - target[None]) - pair_coef * pair_sign)).astype(jnp.bfloat16)

    def back(grad_one):
        return jnp.dot(grad_one.T, weight, preferred_element_type=jnp.float32).astype(jnp.bfloat16)
    grad_hidden = lax.map(back, grad_pred)

    def add_member(total, pair):
        grad_one, rows = pair
        return (total + jnp.dot(grad_one, rows, preferred_element_type=jnp.float32), None)
    grad_weight, _ = lax.scan(add_member, jnp.zeros(weight.shape, jnp.float32), (grad_pred, hidden))
    grad_weight = grad_weight / points
    grad_bias = lax.optimization_barrier(jnp.sum(grad_pred.astype(jnp.float32), axis=(0, 2))) / points
    return (loss, grad_hidden, grad_weight, grad_bias)
```

```python
import functools
import math

import jax
import jax.numpy as jnp
from jax import lax
from jax.experimental import pallas as pl
from jax.experimental.pallas import tpu as pltpu
from jax.sharding import PartitionSpec as P

alpha_fair = 0.95
smooth = 0.3
MESH = pl.DeviceIdType.MESH
F32 = jnp.float32
BF16 = jnp.bfloat16
XL = 2


class Plan:
    def __init__(self, mesh_shape, V, H, G):
        self.E, self.NG = mesh_shape["ens"], mesh_shape["grid"]
        self.V, self.H, self.G = V, H, G
        self.NZ = self.E // XL
        self.VG, self.REM = V // 16, V % 16
        self.NT, self.HC = G // 128, H // 128
        self.FOLD = 16 // self.REM
        self.RT = -(-self.NT // self.FOLD)
        self.FULL = self.VG * self.NT
        self.T = self.FULL + self.RT
        self.TAIL = self.T - self.E
        self.STEP = max(1, self.NZ // max(1, self.TAIL))
        self.PL = XL * self.NG
        self.WF = self.VG * self.HC // 2
        self.NPART = self.WF + -(-(self.REM * self.HC) // 32)
        self.ZR = 32 // self.NZ

    def rank_of(self, e):
        z, xl = e // XL, e % XL
        return jnp.where(xl == z % 2, z, self.NZ + z)

    def owner(self, r):
        z = r % self.NZ
        return z * XL + (r + r // self.NZ) % 2


def kernel(pn, hid_hbm, w_hbm, bias_hbm, tgt_hbm, area_hbm, var_hbm, gp_ref, gw_ref, x_ref,
           hid, w, bias, target, area, var, tgt, scl, varb, bcol, tmp, rem, S, R, G, B, pv, acc,
           xs, X, zx, PP, Q, zs, zr, zo, zg, U, F,
           in_sem, s_send, s_recv, g_send, b_recv, p_send, q_recv, x_send, x_recv, zx_send, zx_recv,
           z_send, z_recv, zg_send, zg_recv, u_send, f_recv):
    E, NG, NZ, VG, REM, NT, HC = pn.E, pn.NG, pn.NZ, pn.VG, pn.REM, pn.NT, pn.HC
    V, FULL, T, TAIL, NPL = pn.V, pn.FULL, pn.T, pn.TAIL, pn.PL
    e = lax.axis_index("ens")
    g = lax.axis_index("grid")
    myz, myx = e // XL, e % XL
    r = pn.rank_of(e)
    q = g * XL + myx

    def plane(k):
        return {"ens": myz * XL + k % XL, "grid": k // XL}

    def column(k):
        return {"ens": k * XL + myx}

    def landed(ref, sem):
        pltpu.make_async_copy(ref, ref, sem).wait()

    ins = [(w_hbm, w), (bias_hbm, bias), (tgt_hbm, target), (area_hbm, area), (var_hbm, var)]
    in_copies = [pltpu.make_async_copy(a, b, in_sem.at[i]) for i, (a, b) in enumerate(ins)]
    hid_copies = [
        pltpu.make_async_copy(hid_hbm.at[pl.ds(t * 128, 128)], hid.at[pl.ds(t * 128, 128)], in_sem.at[len(ins) + t])
        for t in range(NT)
    ]
    in_copies[0].start()
    in_copies[1].start()
    for c in hid_copies:
        c.start()
    for c in in_copies[2:]:
        c.start()

    barrier = pltpu.get_barrier_semaphore()

    @pl.loop(1, E)
    def _(i):
        pl.semaphore_signal(barrier, inc=1, device_id={"ens": lax.rem(e + i, E)}, device_id_type=MESH)

    @pl.loop(1, NPL)
    def _(i):
        pl.semaphore_signal(barrier, inc=1, device_id=plane(lax.rem(q + i, NPL)), device_id_type=MESH)

    in_copies[0].wait()
    in_copies[1].wait()
    varb[...] = jnp.zeros_like(varb)
    varb[:, 0:V] = jnp.broadcast_to(bias[...], (128, V))
    biasb = varb[...].T[0:V]
    rem[...] = jnp.zeros_like(rem)
    for t in range(NT):
        hid_copies[t].wait()
        raw = lax.dot_general(w[...], hid[t * 128:(t + 1) * 128], (((1,), (1,)), ((), ())), preferred_element_type=F32)
        pred = raw + biasb
        for vg in range(VG):
            S[t * VG + vg] = pred[16 * vg:16 * vg + 16].astype(BF16)
        rem[REM * t:REM * t + REM] = pred[16 * VG:V]
    for i in range(pn.RT):
        S[FULL + i] = rem[16 * i:16 * i + 16].astype(BF16)

    pl.semaphore_wait(barrier, E - 1 + NPL - 1)

    def send_tile(slot, j, rank):
        own = pn.owner(rank)

        @pl.when(own == e)
        def _():
            pltpu.make_async_copy(S.at[j], R.at[slot, e], s_recv.at[slot]).start()

        @pl.when(own != e)
        def _():
            pltpu.make_async_remote_copy(
                src_ref=S.at[j], dst_ref=R.at[slot, e], send_sem=s_send.at[slot], recv_sem=s_recv.at[slot],
                device_id={"ens": own}, device_id_type=MESH).start()

    @pl.loop(0, E)
    def _(i):
        rank = lax.rem(r + i, E)
        send_tile(0, rank, rank)

    @pl.loop(0, TAIL)
    def _(i):
        send_tile(1, E + i, i * pn.STEP)

    for c in in_copies[2:]:
        c.wait()
    varb[:, 0:V] = jnp.broadcast_to(var[...], (128, V))
    varb[...] = varb[...].T
    bcol[...] = jnp.zeros_like(bcol)

    tail_i = r // pn.STEP
    has_tail = jnp.logical_and(r % pn.STEP == 0, tail_i < TAIL)

    def prepare(slot, j):
        @pl.when(j < FULL)
        def _():
            vrow = pl.multiple_of((j % VG) * 16, 16)
            col = pl.multiple_of((j // VG) * 128, 128)
            tgt[slot] = target[pl.ds(vrow, 16), pl.ds(col, 128)]
            scl[slot] = varb[pl.ds(vrow, 16)] * area[0:1, pl.ds(col, 128)]

        for i in range(pn.RT):
            @pl.when(j == FULL + i)
            def _():
                tgt[slot] = jnp.zeros((16, 128), F32)
                scl[slot] = jnp.zeros((16, 128), F32)
                for k in range(pn.FOLD):
                    t = i * pn.FOLD + k
                    if t < NT:
                        cols = slice(128 * t, 128 * t + 128)
                        tgt[slot, REM * k:REM * k + REM] = target[16 * VG:V, cols]
                        scl[slot, REM * k:REM * k + REM] = varb[16 * VG:V] * area[0:1, cols]

    prepare(0, r)

    @pl.when(has_tail)
    def _():
        prepare(1, E + tail_i)

    members = E
    eps = (1.0 - alpha_fair) / members
    pair_coef = (1.0 - eps) / (members - 1)
    c2 = smooth * smooth
    BM = min(8, E // 2)
    NB = E // BM

    def blocks(h, i, j, total, diag):
        rows = pl.ds(h * 8, 8)
        a = [pv[i * BM + k, rows] for k in range(BM)]
        b = a if diag else [pv[j * BM + k, rows] for k in range(BM)]
        sa = [acc[i * BM + k, rows] for k in range(BM)]
        sb = sa if diag else [acc[j * BM + k, rows] for k in range(BM)]
        for m in range(BM):
            for k in range(m + 1 if diag else 0, BM):
                d = a[m] - b[k]
                qq = d * d + c2
                rs = lax.rsqrt(qq)
                s = d * rs
                total = total + qq * rs
                sa[m] = sa[m] + s
                sb[k] = sb[k] - s
        for k in range(BM):
            acc[i * BM + k, rows] = sa[k]
            if not diag:
                acc[j * BM + k, rows] = sb[k]
        return total

    def process(slot, j):
        landed(R.at[slot], s_recv.at[slot])

        @pl.loop(0, E)
        def _(m):
            pv[m] = R[slot, m].astype(F32)
            acc[m] = jnp.zeros((16, 128), F32)

        def half(h, _):
            total = lax.fori_loop(0, NB, lambda i, t: blocks(h, i, i, t, True), jnp.zeros((8, 128), F32))

            def off(k, t):
                if NB == 2:
                    return blocks(h, 0, 1, t, False)
                return blocks(h, k % 4, (k + 1 + k // 4) % 4, t, False)
            tmp[pl.ds(h * 8, 8)] = lax.fori_loop(0, NB * (NB - 1) // 2, off, total)
            return 0
        lax.fori_loop(0, 2, half, 0)
        tg, sc = tgt[slot], scl[slot]

        def finish(m, carry):
            bsum, absum = carry
            d = pv[m] - tg
            qq = d * d + c2
            rs = lax.rsqrt(qq)
            gb = (sc * (d * rs - pair_coef * acc[m])).astype(BF16)
            G[slot, m] = gb
            return bsum + gb.astype(F32), absum + qq * rs
        zero = jnp.zeros((16, 128), F32)
        bsum, absum = lax.fori_loop(0, E, finish, (zero, zero))

        @pl.loop(0, E)
        def _(i):
            m = lax.rem(e + i, E)

            @pl.when(m == e)
            def _():
                pltpu.make_async_copy(G.at[slot, m], B.at[j], b_recv).start()

            @pl.when(m != e)
            def _():
                pltpu.make_async_remote_copy(
                    src_ref=G.at[slot, m], dst_ref=B.at[j], send_sem=g_send.at[slot], recv_sem=b_recv,
                    device_id={"ens": m}, device_id_type=MESH).start()

        npair = members * (members - 1) // 2
        crps = (absum - members * smooth) / members - 2.0 * (pair_coef / (2.0 * members)) * (tmp[...] - npair * smooth)
        lossb = jnp.broadcast_to(jnp.sum(sc * crps, axis=(0, 1), keepdims=True), (8, 128))
        bcol[V + 4:V + 12] = bcol[V + 4:V + 12] + lossb
        bb = jnp.broadcast_to(jnp.sum(bsum, axis=1, keepdims=True), (16, 128))

        @pl.when(j < FULL)
        def _():
            rows = pl.ds(pl.multiple_of((j % VG) * 16, 16), 16)
            bcol[rows] = bcol[rows] + bb

        @pl.when(j >= FULL)
        def _():
            tmp[...] = bb
            fold = tmp[0:REM]
            for k in range(1, pn.FOLD):
                fold = fold + tmp[REM * k:REM * k + REM]
            bcol[16 * VG:V] = bcol[16 * VG:V] + fold

    process(0, r)

    @pl.when(has_tail)
    def _():
        process(1, E + tail_i)

    xs[...] = bcol[...].T[0:1]
    X[q] = xs[...]

    @pl.loop(1, NPL)
    def _(i):
        k = lax.rem(q + i, NPL)
        pltpu.make_async_remote_copy(
            src_ref=xs, dst_ref=X.at[q], send_sem=x_send, recv_sem=x_recv, device_id=plane(k), device_id_type=MESH).start()

    landed(B, b_recv)
    for t in range(NT):
        for vg in range(VG):
            gp_ref[16 * vg:16 * vg + 16, 128 * t:128 * t + 128] = B[t * VG + vg]
    for i in range(pn.RT):
        rem[16 * i:16 * i + 16] = B[FULL + i].astype(F32)
    for t in range(NT):
        gp_ref[16 * VG:V, 128 * t:128 * t + 128] = rem[REM * t:REM * t + REM].astype(BF16)

    CW = 256
    for cc in range(pn.H // CW):
        part = lax.dot_general(gp_ref[...], hid[:, cc * CW:(cc + 1) * CW], (((1,), (0,)), ((), ())), preferred_element_type=F32)
        for c2_ in range(CW // 128):
            c = cc * (CW // 128) + c2_
            cols = slice(128 * c2_, 128 * c2_ + 128)
            for vg in range(VG):
                n = c * VG + vg
                PP[n // 2, n % 2] = part[16 * vg:16 * vg + 16, cols].astype(BF16)
            rem[REM * c:REM * c + REM] = part[16 * VG:V, cols]
    for i in range(2):
        PP[pn.WF, i] = rem[16 * i:16 * i + 16].astype(BF16)

    @pl.loop(0, NPL)
    def _(i):
        k = lax.rem(q + i, NPL)

        @pl.when(jnp.logical_and(k < pn.NPART, k == q))
        def _():
            pltpu.make_async_copy(PP.at[k], Q.at[q], q_recv).start()

        @pl.when(jnp.logical_and(k < pn.NPART, k != q))
        def _():
            pltpu.make_async_remote_copy(
                src_ref=PP.at[k], dst_ref=Q.at[q], send_sem=p_send, recv_sem=q_recv,
                device_id=plane(k), device_id_type=MESH).start()

    landed(X.at[pl.ds(0, NPL - 1)], x_recv)
    zx[myz] = lax.fori_loop(1, NPL, lambda i, s: s + X[i], X[0])

    @pl.loop(1, NZ)
    def _(i):
        k = lax.rem(myz + i, NZ)
        pltpu.make_async_remote_copy(
            src_ref=zx.at[myz], dst_ref=zx.at[myz], send_sem=zx_send, recv_sem=zx_recv,
            device_id=column(k), device_id_type=MESH).start()

    points = pn.G * NG

    @pl.when(q < pn.NPART)
    def _():
        landed(Q, q_recv)
        total = lax.fori_loop(0, NPL, lambda i, s: s + Q[i].astype(F32), jnp.zeros((2, 16, 128), F32))
        for i in range(2):
            rem[16 * i:16 * i + 16] = total[i]
        for k in range(NZ):
            zs[k] = rem[pn.ZR * k:pn.ZR * k + pn.ZR]
        zr[myz] = zs[myz]

        @pl.loop(1, NZ)
        def _(i):
            k = lax.rem(myz + i, NZ)
            pltpu.make_async_remote_copy(
                src_ref=zs.at[k], dst_ref=zr.at[myz], send_sem=z_send, recv_sem=z_recv,
                device_id=column(k), device_id_type=MESH).start()
        landed(zr.at[pl.ds(0, NZ - 1)], z_recv)
        zo[...] = lax.fori_loop(0, NZ, lambda i, s: s + zr[i], jnp.zeros((pn.ZR, 128), F32)) * (1.0 / points)
        zg[myz] = zo[...]

        @pl.loop(1, NZ)
        def _(i):
            k = lax.rem(myz + i, NZ)
            pltpu.make_async_remote_copy(
                src_ref=zo, dst_ref=zg.at[myz], send_sem=zg_send, recv_sem=zg_recv,
                device_id=column(k), device_id_type=MESH).start()
        landed(zg.at[pl.ds(0, NZ - 1)], zg_recv)
        for k in range(NZ):
            rem[pn.ZR * k:pn.ZR * k + pn.ZR] = zg[k]
        for i in range(2):
            U[i] = rem[16 * i:16 * i + 16].astype(BF16)

        @pl.loop(0, NPL)
        def _(i):
            k = lax.rem(q + i, NPL)

            @pl.when(k == q)
            def _():
                pltpu.make_async_copy(U, F.at[q], f_recv).start()

            @pl.when(k != q)
            def _():
                pltpu.make_async_remote_copy(
                    src_ref=U, dst_ref=F.at[q], send_sem=u_send, recv_sem=f_recv,
                    device_id=plane(k), device_id_type=MESH).start()

    landed(zx.at[pl.ds(0, NZ - 1)], zx_recv)
    x_ref[...] = lax.fori_loop(0, NZ, lambda i, s: s + zx[i], jnp.zeros((1, 128), F32)) * (1.0 / points)

    landed(F, f_recv)
    for c in range(HC):
        for vg in range(VG):
            n = c * VG + vg
            gw_ref[16 * vg:16 * vg + 16, 128 * c:128 * c + 128] = F[n // 2, n % 2].astype(F32)
    for i in range(2):
        rem[16 * i:16 * i + 16] = F[pn.WF, i].astype(F32)
    for c in range(HC):
        gw_ref[16 * VG:V, 128 * c:128 * c + 128] = rem[REM * c:REM * c + REM]

    landed(S.at[pl.ds(0, E - 1)], s_send.at[0])
    landed(G.at[0, pl.ds(0, E - 1)], g_send.at[0])
    landed(X.at[pl.ds(0, NPL - 1)], x_send)
    landed(zx.at[pl.ds(0, NZ - 1)], zx_send)

    @pl.when(has_tail)
    def _():
        landed(S.at[pl.ds(0, TAIL - 1)], s_send.at[1])
        landed(G.at[1, pl.ds(0, E - 1)], g_send.at[1])

    @pl.when(jnp.logical_not(has_tail))
    def _():
        landed(S.at[pl.ds(0, TAIL)], s_send.at[1])

    @pl.when(q < pn.NPART)
    def _():
        landed(PP.at[pl.ds(0, pn.NPART - 1)], p_send)
        landed(zs.at[pl.ds(0, NZ - 1)], z_send)
        landed(zs.at[pl.ds(0, NZ - 1)], zg_send)
        landed(Q.at[pl.ds(0, NPL - 1)], u_send)

    @pl.when(q >= pn.NPART)
    def _():
        landed(PP, p_send)


def body(mesh_shape, hidden, weight, bias, target, area_weight, var_weight):
    rows = hidden[0]
    V, H = weight.shape
    G = rows.shape[0]
    pn = Plan(mesh_shape, V, H, G)
    E, NZ = pn.E, pn.NZ
    dma = pltpu.SemaphoreType.DMA
    gp, gw, x = pl.pallas_call(
        functools.partial(kernel, pn),
        out_shape=(
            jax.ShapeDtypeStruct((V, G), BF16),
            jax.ShapeDtypeStruct((V, H), F32),
            jax.ShapeDtypeStruct((1, 128), F32),
        ),
        in_specs=[pl.BlockSpec(memory_space=pl.ANY)] * 6,
        out_specs=(pl.BlockSpec(memory_space=pltpu.VMEM),) * 3,
        scratch_shapes=[
            pltpu.VMEM((G, H), BF16),
            pltpu.VMEM((V, H), BF16),
            pltpu.VMEM((1, V), F32),
            pltpu.VMEM((V, G), F32),
            pltpu.VMEM((1, G), F32),
            pltpu.VMEM((1, V), F32),
            pltpu.VMEM((2, 16, 128), F32),
            pltpu.VMEM((2, 16, 128), F32),
            pltpu.VMEM((128, 128), F32),
            pltpu.VMEM((128, 128), F32),
            pltpu.VMEM((16, 128), F32),
            pltpu.VMEM((32, 128), F32),
            pltpu.VMEM((pn.T, 16, 128), BF16),
            pltpu.VMEM((2, E, 16, 128), BF16),
            pltpu.VMEM((2, E, 16, 128), BF16),
            pltpu.VMEM((pn.T, 16, 128), BF16),
            pltpu.VMEM((E, 16, 128), F32),
            pltpu.VMEM((E, 16, 128), F32),
            pltpu.VMEM((1, 128), F32),
            pltpu.VMEM((pn.PL, 1, 128), F32),
            pltpu.VMEM((NZ, 1, 128), F32),
            pltpu.VMEM((pn.NPART, 2, 16, 128), BF16),
            pltpu.VMEM((pn.PL, 2, 16, 128), BF16),
            pltpu.VMEM((NZ, pn.ZR, 128), F32),
            pltpu.VMEM((NZ, pn.ZR, 128), F32),
            pltpu.VMEM((pn.ZR, 128), F32),
            pltpu.VMEM((NZ, pn.ZR, 128), F32),
            pltpu.VMEM((2, 16, 128), BF16),
            pltpu.VMEM((pn.NPART, 2, 16, 128), BF16),
            dma((5 + pn.NT,)),
            dma((2,)),
            dma((2,)),
            dma((2,)),
            dma, dma, dma, dma, dma, dma, dma, dma, dma, dma, dma, dma, dma,
        ],
        compiler_params=pltpu.CompilerParams(
            collective_id=0, has_side_effects=True, vmem_limit_bytes=32 * 1024 * 1024
        ),
        cost_estimate=pl.CostEstimate(flops=4 * V * G * H, bytes_accessed=2 * G * H, transcendentals=V * G * 16),
    )(rows, weight, bias[None], target, area_weight[None], var_weight[None])
    grad_rows = lax.dot_general(gp, weight, (((0,), (0,)), ((), ())), preferred_element_type=F32)
    loss = x[0, V + 4] / V
    grad_bias = x[0, :V]
    return (loss, grad_rows.astype(BF16)[None], gw, grad_bias)


def solution(mesh):
    return jax.shard_map(
        functools.partial(body, dict(mesh.shape)),
        mesh=mesh,
        in_specs=(P("ens", "grid", None), P(), P(), P(None, "grid"), P("grid"), P()),
        out_specs=(P(), P("ens", "grid", None), P(), P()),
        check_vma=False,
    )
```

```python
import functools

import jax
import jax.numpy as jnp
from jax import lax
from jax.experimental import pallas as pl
from jax.experimental.pallas import tpu as pltpu
from jax.sharding import PartitionSpec as P

alpha_fair = 0.95
smooth = 0.3
MESH = pl.DeviceIdType.MESH
F32 = jnp.float32
BF16 = jnp.bfloat16
XL = 2


class Plan:
    def __init__(self, mesh_shape, V, H, G):
        self.E, self.NG = mesh_shape["ens"], mesh_shape["grid"]
        self.V, self.H, self.G = V, H, G
        self.NZ = self.E // XL
        self.VG, self.REM = V // 16, V % 16
        self.NT, self.HC = G // 128, H // 128
        self.FOLD = 16 // self.REM
        self.RT = -(-self.NT // self.FOLD)
        self.FULL = self.VG * self.NT
        self.T = self.FULL + self.RT
        self.TAIL = self.T - self.E
        self.STEP = max(1, self.NZ // max(1, self.TAIL))
        self.PL = XL * self.NG
        mid = self.VG // 2
        self.WAVES = ((0, mid), (mid, self.VG))
        self.RW = -(-(self.REM * self.HC) // 16)
        self.GWT = tuple((b - a) * self.HC + (self.RW if b == self.VG else 0) for a, b in self.WAVES)
        self.GW0 = tuple(sum(self.GWT[:i]) for i in range(len(self.GWT)))
        self.OFF = (0, self.PL - self.GWT[-1])

    def tiles(self, wave):
        a, b = self.WAVES[wave]
        return a * self.NT, self.T if b == self.VG else b * self.NT

    def far_first(self, me, i):
        half = self.NZ // 2
        return (me + half + jnp.where(i % 2 == 1, (i + 1) // 2, self.NZ - i // 2)) % self.NZ

    def rank_of(self, e):
        z, xl = e // XL, e % XL
        return jnp.where(xl == z % 2, z, self.NZ + z)

    def owner(self, r):
        z = r % self.NZ
        return z * XL + (r + r // self.NZ) % 2


def kernel(pn, hid_hbm, w_hbm, bias_hbm, tgt_hbm, area_hbm, var_hbm, gp_ref, f_ref, x_ref,
           hid, w, bias, target, area, var, tgt, scl, varb, bcol, tmp, rem, S, R, G, B, pv, acc,
           xs, X, zx, PP, Q, zs, zr, U, F,
           in_sem, s_send, s_recv, g_send, b_recv, p_send, q_recv, z_send, z_recv, u_send, f_recv,
           x_send, x_recv, zx_send, zx_recv):
    E, NG, NZ, VG, REM, NT, HC = pn.E, pn.NG, pn.NZ, pn.VG, pn.REM, pn.NT, pn.HC
    V, FULL, T, TAIL, NPL = pn.V, pn.FULL, pn.T, pn.TAIL, pn.PL
    NW = len(pn.WAVES)
    e = lax.axis_index("ens")
    g = lax.axis_index("grid")
    myz, myx = e // XL, e % XL
    r = pn.rank_of(e)
    q = g * XL + myx

    def plane(k):
        return {"ens": myz * XL + k % XL, "grid": k // XL}

    def column(k):
        return {"ens": k * XL + myx}

    def landed(ref, sem):
        pltpu.make_async_copy(ref, ref, sem).wait()

    def send(src, dst, send_sem, recv_sem, where):
        pltpu.make_async_remote_copy(
            src_ref=src, dst_ref=dst, send_sem=send_sem, recv_sem=recv_sem, device_id=where, device_id_type=MESH).start()

    barrier = pltpu.get_barrier_semaphore()

    @pl.loop(0, NZ)
    def _(i):
        z = pn.far_first(myz, i)
        for xl in range(XL):
            @pl.when(z * XL + xl != e)
            def _():
                pl.semaphore_signal(barrier, inc=1, device_id={"ens": z * XL + xl}, device_id_type=MESH)

    ins = [(w_hbm, w), (bias_hbm, bias), (tgt_hbm, target), (area_hbm, area), (var_hbm, var)]
    in_copies = [pltpu.make_async_copy(a, b, in_sem.at[i]) for i, (a, b) in enumerate(ins)]
    hid_copies = [
        pltpu.make_async_copy(hid_hbm.at[pl.ds(t * 128, 128)], hid.at[pl.ds(t * 128, 128)], in_sem.at[len(ins) + t])
        for t in range(NT)
    ]
    in_copies[0].start()
    in_copies[1].start()
    for c in hid_copies:
        c.start()
    for c in in_copies[2:]:
        c.start()

    @pl.loop(1, NPL)
    def _(i):
        pl.semaphore_signal(barrier, inc=1, device_id=plane(lax.rem(q + i, NPL)), device_id_type=MESH)

    in_copies[0].wait()
    in_copies[1].wait()
    varb[...] = jnp.zeros_like(varb)
    varb[:, 0:V] = jnp.broadcast_to(bias[...], (128, V))
    biasb = varb[...].T[0:V]
    rem[...] = jnp.zeros_like(rem)
    for t in range(NT):
        hid_copies[t].wait()
        raw = lax.dot_general(w[...], hid[t * 128:(t + 1) * 128], (((1,), (1,)), ((), ())), preferred_element_type=F32)
        pred = raw + biasb
        for vg in range(VG):
            S[vg * NT + t] = pred[16 * vg:16 * vg + 16].astype(BF16)
        rem[REM * t:REM * t + REM] = pred[16 * VG:V]
    for i in range(pn.RT):
        S[FULL + i] = rem[16 * i:16 * i + 16].astype(BF16)

    pl.semaphore_wait(barrier, E - 1 + NPL - 1)

    def send_tile(slot, j, rank):
        own = pn.owner(rank)

        @pl.when(own == e)
        def _():
            pltpu.make_async_copy(S.at[j], R.at[slot, e], s_recv.at[slot]).start()

        @pl.when(own != e)
        def _():
            send(S.at[j], R.at[slot, e], s_send.at[slot], s_recv.at[slot], {"ens": own})

    for wave in range(NW):
        lo, hi = pn.tiles(wave)

        @pl.loop(0, NZ)
        def _(i):
            z = pn.far_first(myz, i)
            for part in range(XL):
                if max(lo, part * NZ) < min(hi, part * NZ + NZ):
                    rank = z + part * NZ

                    @pl.when(jnp.logical_and(rank >= lo, rank < hi))
                    def _():
                        send_tile(0, rank, rank)

    @pl.loop(0, TAIL)
    def _(i):
        send_tile(1, E + i, i * pn.STEP)

    for c in in_copies[2:]:
        c.wait()
    varb[:, 0:V] = jnp.broadcast_to(var[...], (128, V))
    varb[...] = varb[...].T
    bcol[...] = jnp.zeros_like(bcol)

    tail_i = r // pn.STEP
    has_tail = jnp.logical_and(r % pn.STEP == 0, tail_i < TAIL)

    def prepare(slot, j):
        @pl.when(j < FULL)
        def _():
            vrow = pl.multiple_of((j // NT) * 16, 16)
            col = pl.multiple_of((j % NT) * 128, 128)
            tgt[slot] = target[pl.ds(vrow, 16), pl.ds(col, 128)]
            scl[slot] = varb[pl.ds(vrow, 16)] * area[pl.ds(j % NT, 1)]

        for i in range(pn.RT):
            @pl.when(j == FULL + i)
            def _():
                tgt[slot] = jnp.zeros((16, 128), F32)
                scl[slot] = jnp.zeros((16, 128), F32)
                for k in range(pn.FOLD):
                    t = i * pn.FOLD + k
                    if t < NT:
                        cols = slice(128 * t, 128 * t + 128)
                        tgt[slot, REM * k:REM * k + REM] = target[16 * VG:V, cols]
                        scl[slot, REM * k:REM * k + REM] = varb[16 * VG:V] * area[t:t + 1]

    prepare(0, r)

    @pl.when(has_tail)
    def _():
        prepare(1, E + tail_i)

    members = E
    eps = (1.0 - alpha_fair) / members
    pair_coef = (1.0 - eps) / (members - 1)
    c2 = smooth * smooth
    BM = min(8, E // 2)
    NB = E // BM

    def blocks(h, i, j, total, diag):
        rows = pl.ds(h * 8, 8)
        a = [pv[i * BM + k, rows] for k in range(BM)]
        b = a if diag else [pv[j * BM + k, rows] for k in range(BM)]
        sa = [acc[i * BM + k, rows] for k in range(BM)]
        sb = sa if diag else [acc[j * BM + k, rows] for k in range(BM)]
        for m in range(BM):
            for k in range(m + 1 if diag else 0, BM):
                d = a[m] - b[k]
                qq = d * d + c2
                rs = lax.rsqrt(qq)
                s = d * rs
                total = total + qq * rs
                sa[m] = sa[m] + s
                sb[k] = sb[k] - s
        for k in range(BM):
            acc[i * BM + k, rows] = sa[k]
            if not diag:
                acc[j * BM + k, rows] = sb[k]
        return total

    def process(slot, j):
        landed(R.at[slot], s_recv.at[slot])
        for m in range(E):
            pv[m] = R[slot, m].astype(F32)
            acc[m] = jnp.zeros((16, 128), F32)

        def half(h, _):
            total = lax.fori_loop(0, NB, lambda i, t: blocks(h, i, i, t, True), jnp.zeros((8, 128), F32))

            def off(k, t):
                if NB == 2:
                    return blocks(h, 0, 1, t, False)
                return blocks(h, k % 4, (k + 1 + k // 4) % 4, t, False)
            tmp[pl.ds(h * 8, 8)] = lax.fori_loop(0, NB * (NB - 1) // 2, off, total)
            return 0
        lax.fori_loop(0, 2, half, 0)
        tg, sc = tgt[slot], scl[slot]
        wave = jnp.where(j >= pn.tiles(NW - 1)[0], NW - 1, 0)

        def finish(i, carry):
            bsum, absum = carry
            z = pn.far_first(myz, i)
            for xl in range(XL):
                m = z * XL + xl
                d = pv[m] - tg
                qq = d * d + c2
                rs = lax.rsqrt(qq)
                gb = (sc * (d * rs - pair_coef * acc[m])).astype(BF16)
                G[slot, m] = gb
                bsum, absum = bsum + gb.astype(F32), absum + qq * rs

                @pl.when(m == e)
                def _():
                    pltpu.make_async_copy(G.at[slot, m], B.at[j], b_recv.at[wave]).start()

                @pl.when(m != e)
                def _():
                    send(G.at[slot, m], B.at[j], g_send.at[slot], b_recv.at[wave], {"ens": m})
            return bsum, absum
        zero = jnp.zeros((16, 128), F32)
        bsum, absum = lax.fori_loop(0, NZ, finish, (zero, zero))

        npair = members * (members - 1) // 2
        crps = (absum - members * smooth) / members - 2.0 * (pair_coef / (2.0 * members)) * (tmp[...] - npair * smooth)
        lossb = jnp.broadcast_to(jnp.sum(sc * crps, axis=(0, 1), keepdims=True), (8, 128))
        bcol[V + 4:V + 12] = bcol[V + 4:V + 12] + lossb
        bb = jnp.broadcast_to(jnp.sum(bsum, axis=1, keepdims=True), (16, 128))

        @pl.when(j < FULL)
        def _():
            rows = pl.ds(pl.multiple_of((j // NT) * 16, 16), 16)
            bcol[rows] = bcol[rows] + bb

        @pl.when(j >= FULL)
        def _():
            tmp[...] = bb
            fold = tmp[0:REM]
            for k in range(1, pn.FOLD):
                fold = fold + tmp[REM * k:REM * k + REM]
            bcol[16 * VG:V] = bcol[16 * VG:V] + fold

    process(0, r)

    @pl.when(has_tail)
    def _():
        process(1, E + tail_i)

    xs[...] = bcol[...].T[0:1]
    X[q] = xs[...]

    @pl.loop(1, NPL)
    def _(i):
        send(xs, X.at[q], x_send, x_recv, plane(lax.rem(q + i, NPL)))

    def home(wave):
        lo, hi = pn.tiles(wave)
        a, b = pn.WAVES[wave]
        last = b == VG
        landed(B.at[pl.ds(lo, hi - lo)], b_recv.at[wave])
        for t in range(NT):
            for vg in range(a, b):
                gp_ref[16 * vg:16 * vg + 16, 128 * t:128 * t + 128] = B[vg * NT + t]
        if last:
            for i in range(pn.RT):
                rem[16 * i:16 * i + 16] = B[FULL + i].astype(F32)
            for t in range(NT):
                gp_ref[16 * VG:V, 128 * t:128 * t + 128] = rem[REM * t:REM * t + REM].astype(BF16)
        rows = slice(16 * a, V if last else 16 * b)
        CW = 256
        n0 = pn.GW0[wave]
        for cc in range(pn.H // CW):
            part = lax.dot_general(
                gp_ref[rows], hid[:, cc * CW:(cc + 1) * CW], (((1,), (0,)), ((), ())), preferred_element_type=F32)
            for c2_ in range(CW // 128):
                c = cc * (CW // 128) + c2_
                cols = slice(128 * c2_, 128 * c2_ + 128)
                for vg in range(b - a):
                    PP[n0 + c * (b - a) + vg] = part[16 * vg:16 * vg + 16, cols].astype(BF16)
                if last:
                    rem[REM * c:REM * c + REM] = part[16 * (b - a):, cols]
        if last:
            for i in range(pn.RW):
                PP[n0 + HC * (b - a) + i] = rem[16 * i:16 * i + 16].astype(BF16)

        @pl.loop(0, NPL)
        def _(i):
            k = lax.rem(q + i, NPL)
            n = lax.rem(k + NPL - pn.OFF[wave], NPL)

            @pl.when(jnp.logical_and(n < pn.GWT[wave], k == q))
            def _():
                pltpu.make_async_copy(PP.at[n0 + n], Q.at[wave, q], q_recv.at[wave]).start()

            @pl.when(jnp.logical_and(n < pn.GWT[wave], k != q))
            def _():
                send(PP.at[n0 + n], Q.at[wave, q], p_send.at[wave], q_recv.at[wave], plane(k))

    for wave in range(NW):
        home(wave)

    landed(X.at[pl.ds(0, NPL - 1)], x_recv)
    zx[myz] = lax.fori_loop(1, NPL, lambda i, s: s + X[i], X[0])

    @pl.loop(0, NZ - 1)
    def _(i):
        send(zx.at[myz], zx.at[myz], zx_send, zx_recv, column(pn.far_first(myz, i)))

    points = pn.G * NG
    mine = [lax.rem(q + NPL - pn.OFF[wave], NPL) for wave in range(NW)]

    for wave in range(NW):
        @pl.when(mine[wave] < pn.GWT[wave])
        def _():
            landed(Q.at[wave], q_recv.at[wave])
            total = Q[wave, 0].astype(F32)
            for i in range(1, NPL):
                total = total + Q[wave, i].astype(F32)
            zs[wave] = total.astype(BF16)
            zr[wave, myz] = total.astype(BF16)

            @pl.loop(0, NZ - 1)
            def _(i):
                send(zs.at[wave], zr.at[wave, myz], z_send.at[wave], z_recv.at[wave], column(pn.far_first(myz, i)))

    for wave in range(NW):
        @pl.when(mine[wave] < pn.GWT[wave])
        def _():
            landed(zr.at[wave, pl.ds(0, NZ - 1)], z_recv.at[wave])
            total = zr[wave, 0].astype(F32)
            for i in range(1, NZ):
                total = total + zr[wave, i].astype(F32)
            U[wave] = (total * (1.0 / points)).astype(BF16)
            dst = F.at[pn.GW0[wave] + mine[wave]]
            pltpu.make_async_copy(U.at[wave], dst, f_recv.at[wave]).start()

            @pl.loop(1, NPL)
            def _(i):
                send(U.at[wave], dst, u_send.at[wave], f_recv.at[wave], plane(lax.rem(q + i, NPL)))

    landed(zx.at[pl.ds(0, NZ - 1)], zx_recv)
    x_ref[...] = lax.fori_loop(0, NZ, lambda i, s: s + zx[i], jnp.zeros((1, 128), F32)) * (1.0 / points)

    landed(S.at[pl.ds(0, E - 1)], s_send.at[0])
    landed(G.at[0, pl.ds(0, E - 1)], g_send.at[0])
    landed(X.at[pl.ds(0, NPL - 1)], x_send)
    landed(zx.at[pl.ds(0, NZ - 1)], zx_send)

    @pl.when(has_tail)
    def _():
        landed(S.at[pl.ds(0, TAIL - 1)], s_send.at[1])
        landed(G.at[1, pl.ds(0, E - 1)], g_send.at[1])

    @pl.when(jnp.logical_not(has_tail))
    def _():
        landed(S.at[pl.ds(0, TAIL)], s_send.at[1])

    for wave in range(NW):
        n = pn.GWT[wave]

        @pl.when(mine[wave] < n)
        def _():
            landed(PP.at[pl.ds(0, n - 1)], p_send.at[wave])
            landed(zr.at[wave, pl.ds(0, NZ - 1)], z_send.at[wave])
            landed(Q.at[wave, pl.ds(0, NPL - 1)], u_send.at[wave])

        @pl.when(mine[wave] >= n)
        def _():
            landed(PP.at[pl.ds(0, n)], p_send.at[wave])

    for wave in range(NW):
        n0, n = pn.GW0[wave], pn.GWT[wave]
        landed(F.at[pl.ds(n0, n)], f_recv.at[wave])
        f_ref[n0:n0 + n] = F[n0:n0 + n]


def finish_kernel(pn, gp, w, f, x, loss_ref, gh_hbm, gw_hbm, gb_ref, gw, gh, rem, sems):
    V, VG, REM, HC = pn.V, pn.VG, pn.REM, pn.HC
    for wave, (a, b) in enumerate(pn.WAVES):
        for c in range(HC):
            for vg in range(a, b):
                gw[16 * vg:16 * vg + 16, 128 * c:128 * c + 128] = f[pn.GW0[wave] + c * (b - a) + vg - a].astype(F32)
    for i in range(pn.RW):
        rem[16 * i:16 * i + 16] = f[pn.GW0[-1] + pn.GWT[-1] - pn.RW + i].astype(F32)
    for c in range(HC):
        gw[16 * VG:V, 128 * c:128 * c + 128] = rem[REM * c:REM * c + REM]
    copies = [pltpu.make_async_copy(gw, gw_hbm, sems.at[0])]
    copies[0].start()
    for t in range(pn.NT):
        rows = slice(128 * t, 128 * t + 128)
        gh[rows] = lax.dot_general(
            gp[:, rows], w[...], (((0,), (0,)), ((), ())), preferred_element_type=F32).astype(BF16)
        out = pltpu.make_async_copy(gh.at[pl.ds(128 * t, 128)], gh_hbm.at[pl.ds(128 * t, 128)], sems.at[1 + t])
        out.start()
        copies.append(out)
    gb_ref[...] = x[0:1, 0:V]
    loss_ref[...] = x[0:1, V + 4:V + 5] * (1.0 / V)
    for out in copies:
        out.wait()


def body(mesh_shape, hidden, weight, bias, target, area_weight, var_weight):
    rows = hidden[0]
    V, H = weight.shape
    G = rows.shape[0]
    pn = Plan(mesh_shape, V, H, G)
    E, NZ = pn.E, pn.NZ
    NW = len(pn.WAVES)
    tile = (16, 128)
    NF = sum(pn.GWT)
    dma = pltpu.SemaphoreType.DMA
    vmem = pl.BlockSpec(memory_space=pltpu.VMEM)
    anywhere = pl.BlockSpec(memory_space=pl.ANY)
    gp, f, x = pl.pallas_call(
        functools.partial(kernel, pn),
        out_shape=(
            jax.ShapeDtypeStruct((V, G), BF16),
            jax.ShapeDtypeStruct((NF,) + tile, BF16),
            jax.ShapeDtypeStruct((1, 128), F32),
        ),
        in_specs=[anywhere] * 6,
        out_specs=(vmem,) * 3,
        scratch_shapes=[
            pltpu.VMEM((G, H), BF16),
            pltpu.VMEM((V, H), BF16),
            pltpu.VMEM((1, V), F32),
            pltpu.VMEM((V, G), F32),
            pltpu.VMEM((pn.NT, 128), F32),
            pltpu.VMEM((1, V), F32),
            pltpu.VMEM((2,) + tile, F32),
            pltpu.VMEM((2,) + tile, F32),
            pltpu.VMEM((128, 128), F32),
            pltpu.VMEM((128, 128), F32),
            pltpu.VMEM(tile, F32),
            pltpu.VMEM((32, 128), F32),
            pltpu.VMEM((pn.T,) + tile, BF16),
            pltpu.VMEM((2, E) + tile, BF16),
            pltpu.VMEM((2, E) + tile, BF16),
            pltpu.VMEM((pn.T,) + tile, BF16),
            pltpu.VMEM((E,) + tile, F32),
            pltpu.VMEM((E,) + tile, F32),
            pltpu.VMEM((1, 128), F32),
            pltpu.VMEM((pn.PL, 1, 128), F32),
            pltpu.VMEM((NZ, 1, 128), F32),
            pltpu.VMEM((NF,) + tile, BF16),
            pltpu.VMEM((NW, pn.PL) + tile, BF16),
            pltpu.VMEM((NW,) + tile, BF16),
            pltpu.VMEM((NW, NZ) + tile, BF16),
            pltpu.VMEM((NW,) + tile, BF16),
            pltpu.VMEM((NF,) + tile, BF16),
            dma((5 + pn.NT,)),
            dma((2,)),
            dma((2,)),
            dma((2,)),
            dma((NW,)),
            dma((NW,)),
            dma((NW,)),
            dma((NW,)),
            dma((NW,)),
            dma((NW,)),
            dma((NW,)),
            dma, dma, dma, dma,
        ],
        compiler_params=pltpu.CompilerParams(
            collective_id=0, has_side_effects=True, vmem_limit_bytes=60 * 1024 * 1024
        ),
        cost_estimate=pl.CostEstimate(flops=4 * V * G * H, bytes_accessed=2 * G * H, transcendentals=V * G * 16),
    )(rows, weight, bias[None], target, area_weight.reshape(-1, 128), var_weight[None])
    loss, gh, gw, gb = pl.pallas_call(
        functools.partial(finish_kernel, pn),
        out_shape=(
            jax.ShapeDtypeStruct((1, 1), F32),
            jax.ShapeDtypeStruct((G, H), BF16),
            jax.ShapeDtypeStruct((V, H), F32),
            jax.ShapeDtypeStruct((1, V), F32),
        ),
        in_specs=[vmem] * 4,
        out_specs=(vmem, anywhere, anywhere, vmem),
        scratch_shapes=[
            pltpu.VMEM((V, H), F32),
            pltpu.VMEM((G, H), BF16),
            pltpu.VMEM((32, 128), F32),
            dma((1 + pn.NT,)),
        ],
        compiler_params=pltpu.CompilerParams(vmem_limit_bytes=60 * 1024 * 1024),
        cost_estimate=pl.CostEstimate(flops=2 * V * G * H, bytes_accessed=2 * G * H, transcendentals=0),
    )(gp, weight, f, x)
    return (loss[0, 0], gh[None], gw, gb[0])


def solution(mesh):
    return jax.shard_map(
        functools.partial(body, dict(mesh.shape)),
        mesh=mesh,
        in_specs=(P("ens", "grid", None), P(), P(), P(None, "grid"), P("grid"), P()),
        out_specs=(P(), P("ens", "grid", None), P(), P()),
        check_vma=False,
    )
```

```python
import functools

import jax
import jax.numpy as jnp
from jax import lax
from jax.experimental import pallas as pl
from jax.experimental.pallas import tpu as pltpu
from jax.sharding import PartitionSpec as P

alpha_fair = 0.95
smooth = 0.3
MESH = pl.DeviceIdType.MESH
F32 = jnp.float32
BF16 = jnp.bfloat16
XL = 2


class Plan:
    def __init__(self, mesh_shape, V, H, G):
        self.E, self.NG = mesh_shape["ens"], mesh_shape["grid"]
        self.V, self.H, self.G = V, H, G
        self.NZ = self.E // XL
        self.VG, self.REM = V // 16, V % 16
        self.NT, self.HC = G // 128, H // 128
        self.FOLD = 16 // self.REM
        self.RT = -(-self.NT // self.FOLD)
        self.FULL = self.VG * self.NT
        self.T = self.FULL + self.RT
        self.TAIL = self.T - self.E
        self.STEP = max(1, self.NZ // max(1, self.TAIL))
        self.PL = XL * self.NG
        nw = min(2, self.VG)
        cuts = [self.VG * i // nw for i in range(nw + 1)]
        self.WAVES = tuple(zip(cuts[:-1], cuts[1:]))
        self.RW = -(-(self.REM * self.HC) // 16)
        self.GWT = tuple((b - a) * self.HC + (self.RW if b == self.VG else 0) for a, b in self.WAVES)
        self.GW0 = tuple(sum(self.GWT[:i]) for i in range(len(self.GWT)))

    def tiles(self, wave):
        a, b = self.WAVES[wave]
        return a * self.NT, self.T if b == self.VG else b * self.NT

    def wave_of(self, j):
        wave = 0
        for k in range(1, len(self.WAVES)):
            wave = wave + jnp.where(j >= self.tiles(k)[0], 1, 0)
        return wave

    def owned(self, q, wave):
        return q // 4 * 2 + q % 2 + self.PL // 2 * ((q // 2 + wave) % 2)

    def plane_peer(self, q, i):
        return lax.rem(q + 1 + i, self.PL)

    def far_first(self, me, i):
        half = self.NZ // 2
        return (me + half + jnp.where(i % 2 == 1, (i + 1) // 2, self.NZ - i // 2)) % self.NZ

    def rank_of(self, e):
        z, xl = e // XL, e % XL
        return jnp.where(xl == z % 2, z, self.NZ + z)

    def owner(self, r):
        z = r % self.NZ
        return z * XL + (r + r // self.NZ) % 2


def kernel(pn, hid_hbm, w_hbm, bias_hbm, tgt_hbm, area_hbm, var_hbm, gp_hbm, f_hbm, x_ref,
           gp_ref, hid, w, bias, target, area, var, tgt, scl, varb, bcol, tmp, rem, S, R, G, B, pv, acc,
           xs, X, zx, PP, Q, zs, zr, U, F,
           in_sem, s_send, s_recv, g_send, b_recv, p_send, q_recv, z_send, z_recv, u_send, f_recv,
           out_sem, x_send, x_recv, zx_send, zx_recv):
    E, NG, NZ, VG, REM, NT, HC = pn.E, pn.NG, pn.NZ, pn.VG, pn.REM, pn.NT, pn.HC
    V, FULL, T, TAIL, NPL = pn.V, pn.FULL, pn.T, pn.TAIL, pn.PL
    NW = len(pn.WAVES)
    e = lax.axis_index("ens")
    g = lax.axis_index("grid")
    myz, myx = e // XL, e % XL
    r = pn.rank_of(e)
    q = g * XL + myx

    def plane(k):
        return {"ens": myz * XL + k % XL, "grid": k // XL}

    def column(k):
        return {"ens": k * XL + myx}

    def landed(ref, sem):
        pltpu.make_async_copy(ref, ref, sem).wait()

    def send(src, dst, send_sem, recv_sem, where):
        pltpu.make_async_remote_copy(
            src_ref=src, dst_ref=dst, send_sem=send_sem, recv_sem=recv_sem, device_id=where, device_id_type=MESH).start()

    barrier = pltpu.get_barrier_semaphore()

    @pl.loop(0, NZ)
    def _(i):
        z = pn.far_first(myz, i)
        for xl in range(XL):
            @pl.when(z * XL + xl != e)
            def _():
                pl.semaphore_signal(barrier, inc=1, device_id={"ens": z * XL + xl}, device_id_type=MESH)

    ins = [(w_hbm, w), (bias_hbm, bias), (tgt_hbm, target), (area_hbm, area), (var_hbm, var)]
    in_copies = [pltpu.make_async_copy(a, b, in_sem.at[i]) for i, (a, b) in enumerate(ins)]
    hid_copies = [
        pltpu.make_async_copy(hid_hbm.at[pl.ds(t * 128, 128)], hid.at[pl.ds(t * 128, 128)], in_sem.at[len(ins) + t])
        for t in range(NT)
    ]
    in_copies[0].start()
    in_copies[1].start()
    for c in hid_copies:
        c.start()
    for c in in_copies[2:]:
        c.start()

    @pl.loop(0, NPL - 1)
    def _(i):
        pl.semaphore_signal(barrier, inc=1, device_id=plane(pn.plane_peer(q, i)), device_id_type=MESH)

    in_copies[0].wait()
    in_copies[1].wait()
    varb[...] = jnp.zeros_like(varb)
    varb[:, 0:V] = jnp.broadcast_to(bias[...], (128, V))
    biasb = varb[...].T[0:V]
    rem[...] = jnp.zeros_like(rem)
    for t in range(NT):
        hid_copies[t].wait()
        raw = lax.dot_general(w[...], hid[t * 128:(t + 1) * 128], (((1,), (1,)), ((), ())), preferred_element_type=F32)
        pred = raw + biasb
        for vg in range(VG):
            S[vg * NT + t] = pred[16 * vg:16 * vg + 16].astype(BF16)
        rem[REM * t:REM * t + REM] = pred[16 * VG:V]
    for i in range(pn.RT):
        S[FULL + i] = rem[16 * i:16 * i + 16].astype(BF16)

    pl.semaphore_wait(barrier, E - 1 + NPL - 1)

    def send_tile(slot, j, rank):
        own = pn.owner(rank)

        @pl.when(own == e)
        def _():
            pltpu.make_async_copy(S.at[j], R.at[slot, e], s_recv.at[slot]).start()

        @pl.when(own != e)
        def _():
            send(S.at[j], R.at[slot, e], s_send.at[slot], s_recv.at[slot], {"ens": own})

    for wave in range(NW):
        lo, hi = pn.tiles(wave)

        @pl.loop(0, NZ)
        def _(i):
            z = pn.far_first(myz, i)
            for part in range(XL):
                if max(lo, part * NZ) < min(hi, part * NZ + NZ):
                    rank = z + part * NZ

                    @pl.when(jnp.logical_and(rank >= lo, rank < hi))
                    def _():
                        send_tile(0, rank, rank)

    @pl.loop(0, TAIL)
    def _(i):
        send_tile(1, E + i, i * pn.STEP)

    for c in in_copies[2:]:
        c.wait()
    varb[:, 0:V] = jnp.broadcast_to(var[...], (128, V))
    varb[...] = varb[...].T
    bcol[...] = jnp.zeros_like(bcol)

    tail_i = r // pn.STEP
    has_tail = jnp.logical_and(r % pn.STEP == 0, tail_i < TAIL)

    def prepare(slot, j):
        @pl.when(j < FULL)
        def _():
            vrow = pl.multiple_of((j // NT) * 16, 16)
            col = pl.multiple_of((j % NT) * 128, 128)
            tgt[slot] = target[pl.ds(vrow, 16), pl.ds(col, 128)]
            scl[slot] = varb[pl.ds(vrow, 16)] * area[pl.ds(j % NT, 1)]

        for i in range(pn.RT):
            @pl.when(j == FULL + i)
            def _():
                tgt[slot] = jnp.zeros((16, 128), F32)
                scl[slot] = jnp.zeros((16, 128), F32)
                for k in range(pn.FOLD):
                    t = i * pn.FOLD + k
                    if t < NT:
                        cols = slice(128 * t, 128 * t + 128)
                        tgt[slot, REM * k:REM * k + REM] = target[16 * VG:V, cols]
                        scl[slot, REM * k:REM * k + REM] = varb[16 * VG:V] * area[t:t + 1]

    prepare(0, r)

    @pl.when(has_tail)
    def _():
        prepare(1, E + tail_i)

    members = E
    eps = (1.0 - alpha_fair) / members
    pair_coef = (1.0 - eps) / (members - 1)
    c2 = smooth * smooth
    BM = E // 2

    def blocks(h, i, j, total, diag):
        rows = pl.ds(h * 8, 8)
        a = [pv[i * BM + k, rows] for k in range(BM)]
        b = a if diag else [pv[j * BM + k, rows] for k in range(BM)]
        sa = [acc[i * BM + k, rows] for k in range(BM)]
        sb = sa if diag else [acc[j * BM + k, rows] for k in range(BM)]
        for m in range(BM):
            for k in range(m + 1 if diag else 0, BM):
                d = a[m] - b[k]
                qq = d * d + c2
                rs = lax.rsqrt(qq)
                s = d * rs
                total = total + qq * rs
                sa[m] = sa[m] + s
                sb[k] = sb[k] - s
        for k in range(BM):
            acc[i * BM + k, rows] = sa[k]
            if not diag:
                acc[j * BM + k, rows] = sb[k]
        return total

    def process(slot, j):
        landed(R.at[slot], s_recv.at[slot])
        for m in range(E):
            pv[m] = R[slot, m].astype(F32)
            acc[m] = jnp.zeros((16, 128), F32)

        @pl.loop(0, 2)
        def _(h):
            total = blocks(h, 0, 0, jnp.zeros((8, 128), F32), True)
            total = blocks(h, 1, 1, total, True)
            tmp[pl.ds(h * 8, 8)] = blocks(h, 0, 1, total, False)
        tg, sc = tgt[slot], scl[slot]
        wave = pn.wave_of(j)

        def finish(i, carry):
            bsum, absum = carry
            z = pn.far_first(myz, i)
            for xl in range(XL):
                m = z * XL + xl
                d = pv[m] - tg
                qq = d * d + c2
                rs = lax.rsqrt(qq)
                gb = (sc * (d * rs - pair_coef * acc[m])).astype(BF16)
                G[slot, m] = gb
                bsum, absum = bsum + gb.astype(F32), absum + qq * rs

                @pl.when(m == e)
                def _():
                    pltpu.make_async_copy(G.at[slot, m], B.at[j], b_recv.at[wave]).start()

                @pl.when(m != e)
                def _():
                    send(G.at[slot, m], B.at[j], g_send.at[slot], b_recv.at[wave], {"ens": m})
            return bsum, absum
        zero = jnp.zeros((16, 128), F32)
        bsum, absum = lax.fori_loop(0, NZ, finish, (zero, zero))

        npair = members * (members - 1) // 2
        crps = (absum - members * smooth) / members - 2.0 * (pair_coef / (2.0 * members)) * (tmp[...] - npair * smooth)
        lossb = jnp.broadcast_to(jnp.sum(sc * crps, axis=(0, 1), keepdims=True), (8, 128))
        bcol[V + 4:V + 12] = bcol[V + 4:V + 12] + lossb
        bb = jnp.broadcast_to(jnp.sum(bsum, axis=1, keepdims=True), (16, 128))

        @pl.when(j < FULL)
        def _():
            rows = pl.ds(pl.multiple_of((j // NT) * 16, 16), 16)
            bcol[rows] = bcol[rows] + bb

        @pl.when(j >= FULL)
        def _():
            tmp[...] = bb
            fold = tmp[0:REM]
            for k in range(1, pn.FOLD):
                fold = fold + tmp[REM * k:REM * k + REM]
            bcol[16 * VG:V] = bcol[16 * VG:V] + fold

    @pl.loop(0, 2)
    def _(slot):
        @pl.when(jnp.logical_or(slot == 0, has_tail))
        def _():
            process(slot, jnp.where(slot == 0, r, E + tail_i))

    xs[...] = bcol[...].T[0:1]
    X[q] = xs[...]

    @pl.loop(0, NPL - 1)
    def _(i):
        send(xs, X.at[q], x_send, x_recv, plane(pn.plane_peer(q, i)))

    def home(wave):
        lo, hi = pn.tiles(wave)
        a, b = pn.WAVES[wave]
        last = b == VG
        landed(B.at[pl.ds(lo, hi - lo)], b_recv.at[wave])
        for t in range(NT):
            for vg in range(a, b):
                gp_ref[16 * vg:16 * vg + 16, 128 * t:128 * t + 128] = B[vg * NT + t]
        if last:
            for i in range(pn.RT):
                rem[16 * i:16 * i + 16] = B[FULL + i].astype(F32)
            for t in range(NT):
                gp_ref[16 * VG:V, 128 * t:128 * t + 128] = rem[REM * t:REM * t + REM].astype(BF16)
        rows = slice(16 * a, V if last else 16 * b)
        CW = 256
        n0 = pn.GW0[wave]
        for cc in range(pn.H // CW):
            part = lax.dot_general(
                gp_ref[rows], hid[:, cc * CW:(cc + 1) * CW], (((1,), (0,)), ((), ())), preferred_element_type=F32)
            for c2_ in range(CW // 128):
                c = cc * (CW // 128) + c2_
                cols = slice(128 * c2_, 128 * c2_ + 128)
                for vg in range(b - a):
                    PP[n0 + c * (b - a) + vg] = part[16 * vg:16 * vg + 16, cols].astype(BF16)
                if last:
                    rem[REM * c:REM * c + REM] = part[16 * (b - a):, cols]
        if last:
            for i in range(pn.RW):
                PP[n0 + HC * (b - a) + i] = rem[16 * i:16 * i + 16].astype(BF16)

        @pl.loop(0, NPL)
        def _(i):
            k = pn.plane_peer(q, i)
            n = pn.owned(k, wave)

            @pl.when(jnp.logical_and(n < pn.GWT[wave], k == q))
            def _():
                pltpu.make_async_copy(PP.at[n0 + n], Q.at[wave, q], q_recv.at[wave]).start()

            @pl.when(jnp.logical_and(n < pn.GWT[wave], k != q))
            def _():
                send(PP.at[n0 + n], Q.at[wave, q], p_send.at[wave], q_recv.at[wave], plane(k))

    for wave in range(NW):
        home(wave)
    out_copies = [pltpu.make_async_copy(gp_ref, gp_hbm, out_sem.at[0])]
    out_copies[0].start()

    landed(X.at[pl.ds(0, NPL - 1)], x_recv)
    zx[myz] = lax.fori_loop(1, NPL, lambda i, s: s + X[i], X[0])

    @pl.loop(0, NZ - 1)
    def _(i):
        send(zx.at[myz], zx.at[myz], zx_send, zx_recv, column(pn.far_first(myz, i)))

    points = pn.G * NG
    mine = [pn.owned(q, wave) for wave in range(NW)]

    for wave in range(NW):
        @pl.when(mine[wave] < pn.GWT[wave])
        def _():
            landed(Q.at[wave], q_recv.at[wave])
            total = Q[wave, 0].astype(F32)
            for i in range(1, NPL):
                total = total + Q[wave, i].astype(F32)
            zs[wave] = total.astype(BF16)
            zr[wave, myz] = total.astype(BF16)

            @pl.loop(0, NZ - 1)
            def _(i):
                send(zs.at[wave], zr.at[wave, myz], z_send.at[wave], z_recv.at[wave], column(pn.far_first(myz, i)))

    for wave in range(NW):
        @pl.when(mine[wave] < pn.GWT[wave])
        def _():
            landed(zr.at[wave, pl.ds(0, NZ - 1)], z_recv.at[wave])
            total = zr[wave, 0].astype(F32)
            for i in range(1, NZ):
                total = total + zr[wave, i].astype(F32)
            U[wave] = (total * (1.0 / points)).astype(BF16)
            dst = F.at[pn.GW0[wave] + mine[wave]]
            pltpu.make_async_copy(U.at[wave], dst, f_recv.at[wave]).start()

            @pl.loop(0, NPL - 1)
            def _(i):
                send(U.at[wave], dst, u_send.at[wave], f_recv.at[wave], plane(pn.plane_peer(q, i)))

    landed(zx.at[pl.ds(0, NZ - 1)], zx_recv)
    x_ref[...] = lax.fori_loop(0, NZ, lambda i, s: s + zx[i], jnp.zeros((1, 128), F32)) * (1.0 / points)

    landed(S.at[pl.ds(0, E - 1)], s_send.at[0])
    landed(G.at[0, pl.ds(0, E - 1)], g_send.at[0])
    landed(X.at[pl.ds(0, NPL - 1)], x_send)
    landed(zx.at[pl.ds(0, NZ - 1)], zx_send)

    @pl.when(has_tail)
    def _():
        landed(S.at[pl.ds(0, TAIL - 1)], s_send.at[1])
        landed(G.at[1, pl.ds(0, E - 1)], g_send.at[1])

    @pl.when(jnp.logical_not(has_tail))
    def _():
        landed(S.at[pl.ds(0, TAIL)], s_send.at[1])

    for wave in range(NW):
        n = pn.GWT[wave]

        @pl.when(mine[wave] < n)
        def _():
            landed(PP.at[pl.ds(0, n - 1)], p_send.at[wave])
            landed(zr.at[wave, pl.ds(0, NZ - 1)], z_send.at[wave])
            landed(Q.at[wave, pl.ds(0, NPL - 1)], u_send.at[wave])

        @pl.when(mine[wave] >= n)
        def _():
            landed(PP.at[pl.ds(0, n)], p_send.at[wave])

    for wave in range(NW):
        n0, n = pn.GW0[wave], pn.GWT[wave]
        landed(F.at[pl.ds(n0, n)], f_recv.at[wave])
        out_copies.append(pltpu.make_async_copy(F.at[pl.ds(n0, n)], f_hbm.at[pl.ds(n0, n)], out_sem.at[1 + wave]))
        out_copies[-1].start()
    for c in out_copies:
        c.wait()


def finish_kernel(pn, gp, w, f, x, loss_ref, gh_hbm, gw_hbm, gb_ref, gw, gh, rem, sems):
    V, VG, REM, HC = pn.V, pn.VG, pn.REM, pn.HC
    for wave, (a, b) in enumerate(pn.WAVES):
        for c in range(HC):
            for vg in range(a, b):
                gw[16 * vg:16 * vg + 16, 128 * c:128 * c + 128] = f[pn.GW0[wave] + c * (b - a) + vg - a].astype(F32)
    for i in range(pn.RW):
        rem[16 * i:16 * i + 16] = f[pn.GW0[-1] + pn.GWT[-1] - pn.RW + i].astype(F32)
    for c in range(HC):
        gw[16 * VG:V, 128 * c:128 * c + 128] = rem[REM * c:REM * c + REM]
    copies = [pltpu.make_async_copy(gw, gw_hbm, sems.at[0])]
    copies[0].start()
    for t in range(pn.NT):
        rows = slice(128 * t, 128 * t + 128)
        gh[rows] = lax.dot_general(
            gp[:, rows], w[...], (((0,), (0,)), ((), ())), preferred_element_type=F32).astype(BF16)
        out = pltpu.make_async_copy(gh.at[pl.ds(128 * t, 128)], gh_hbm.at[pl.ds(128 * t, 128)], sems.at[1 + t])
        out.start()
        copies.append(out)
    gb_ref[...] = x[0:1, 0:V]
    loss_ref[...] = x[0:1, V + 4:V + 5] * (1.0 / V)
    for out in copies:
        out.wait()


def body(mesh_shape, hidden, weight, bias, target, area_weight, var_weight):
    rows = hidden[0]
    V, H = weight.shape
    G = rows.shape[0]
    pn = Plan(mesh_shape, V, H, G)
    E, NZ = pn.E, pn.NZ
    NW = len(pn.WAVES)
    tile = (16, 128)
    NF = sum(pn.GWT)
    dma = pltpu.SemaphoreType.DMA
    vmem = pl.BlockSpec(memory_space=pltpu.VMEM)
    anywhere = pl.BlockSpec(memory_space=pl.ANY)
    gp, f, x = pl.pallas_call(
        functools.partial(kernel, pn),
        out_shape=(
            jax.ShapeDtypeStruct((V, G), BF16),
            jax.ShapeDtypeStruct((NF,) + tile, BF16),
            jax.ShapeDtypeStruct((1, 128), F32),
        ),
        in_specs=[anywhere] * 6,
        out_specs=(anywhere, anywhere, vmem),
        scratch_shapes=[
            pltpu.VMEM((V, G), BF16),
            pltpu.VMEM((G, H), BF16),
            pltpu.VMEM((V, H), BF16),
            pltpu.VMEM((1, V), F32),
            pltpu.VMEM((V, G), F32),
            pltpu.VMEM((pn.NT, 128), F32),
            pltpu.VMEM((1, V), F32),
            pltpu.VMEM((2,) + tile, F32),
            pltpu.VMEM((2,) + tile, F32),
            pltpu.VMEM((128, 128), F32),
            pltpu.VMEM((128, 128), F32),
            pltpu.VMEM(tile, F32),
            pltpu.VMEM((32, 128), F32),
            pltpu.VMEM((pn.T,) + tile, BF16),
            pltpu.VMEM((2, E) + tile, BF16),
            pltpu.VMEM((2, E) + tile, BF16),
            pltpu.VMEM((pn.T,) + tile, BF16),
            pltpu.VMEM((E,) + tile, F32),
            pltpu.VMEM((E,) + tile, F32),
            pltpu.VMEM((1, 128), F32),
            pltpu.VMEM((pn.PL, 1, 128), F32),
            pltpu.VMEM((NZ, 1, 128), F32),
            pltpu.VMEM((NF,) + tile, BF16),
            pltpu.VMEM((NW, pn.PL) + tile, BF16),
            pltpu.VMEM((NW,) + tile, BF16),
            pltpu.VMEM((NW, NZ) + tile, BF16),
            pltpu.VMEM((NW,) + tile, BF16),
            pltpu.VMEM((NF,) + tile, BF16),
            dma((5 + pn.NT,)),
            dma((2,)),
            dma((2,)),
            dma((2,)),
            dma((NW,)),
            dma((NW,)),
            dma((NW,)),
            dma((NW,)),
            dma((NW,)),
            dma((NW,)),
            dma((NW,)),
            dma((1 + NW,)),
            dma, dma, dma, dma,
        ],
        compiler_params=pltpu.CompilerParams(
            collective_id=0, has_side_effects=True, vmem_limit_bytes=60 * 1024 * 1024
        ),
        cost_estimate=pl.CostEstimate(flops=4 * V * G * H, bytes_accessed=2 * G * H, transcendentals=V * G * 16),
    )(rows, weight, bias[None], target, area_weight.reshape(-1, 128), var_weight[None])
    loss, gh, gw, gb = pl.pallas_call(
        functools.partial(finish_kernel, pn),
        out_shape=(
            jax.ShapeDtypeStruct((1, 1), F32),
            jax.ShapeDtypeStruct((G, H), BF16),
            jax.ShapeDtypeStruct((V, H), F32),
            jax.ShapeDtypeStruct((1, V), F32),
        ),
        in_specs=[vmem] * 4,
        out_specs=(vmem, anywhere, anywhere, vmem),
        scratch_shapes=[
            pltpu.VMEM((V, H), F32),
            pltpu.VMEM((G, H), BF16),
            pltpu.VMEM((32, 128), F32),
            dma((1 + pn.NT,)),
        ],
        compiler_params=pltpu.CompilerParams(vmem_limit_bytes=60 * 1024 * 1024),
        cost_estimate=pl.CostEstimate(flops=2 * V * G * H, bytes_accessed=2 * G * H, transcendentals=0),
    )(gp, weight, f, x)
    return (loss[0, 0], gh[None], gw, gb[0])


def solution(mesh):
    return jax.shard_map(
        functools.partial(body, dict(mesh.shape)),
        mesh=mesh,
        in_specs=(P("ens", "grid", None), P(), P(), P(None, "grid"), P("grid"), P()),
        out_specs=(P(), P("ens", "grid", None), P(), P()),
        check_vma=False,
    )
```

```python
import functools

import jax
import jax.numpy as jnp
from jax import lax
from jax.experimental import pallas as pl
from jax.experimental.pallas import tpu as pltpu
from jax.sharding import PartitionSpec as P

alpha_fair = 0.95
smooth = 0.3
MESH = pl.DeviceIdType.MESH
F32 = jnp.float32
BF16 = jnp.bfloat16
XL = 2


class Plan:
    def __init__(self, mesh_shape, V, H, G):
        self.E, self.NG = mesh_shape["ens"], mesh_shape["grid"]
        self.V, self.H, self.G = V, H, G
        self.NZ = self.E // XL
        self.VG, self.REM = V // 16, V % 16
        self.NT, self.HC = G // 128, H // 128
        self.FOLD = 16 // self.REM
        self.RT = -(-self.NT // self.FOLD)
        self.FULL = self.VG * self.NT
        self.T = self.FULL + self.RT
        self.TAIL = self.T - self.E
        self.STEP = max(1, self.NZ // max(1, self.TAIL))
        self.PL = XL * self.NG
        nw = min(2, self.VG)
        cuts = [self.VG * i // nw for i in range(nw + 1)]
        self.WAVES = tuple(zip(cuts[:-1], cuts[1:]))
        self.RW = -(-(self.REM * self.HC) // 16)
        self.GWT = tuple((b - a) * self.HC + (self.RW if b == self.VG else 0) for a, b in self.WAVES)
        self.GW0 = tuple(sum(self.GWT[:i]) for i in range(len(self.GWT)))

    def tiles(self, wave):
        a, b = self.WAVES[wave]
        return a * self.NT, self.T if b == self.VG else b * self.NT

    def wave_of(self, j):
        wave = 0
        for k in range(1, len(self.WAVES)):
            wave = wave + jnp.where(j >= self.tiles(k)[0], 1, 0)
        return wave

    def owned(self, q, wave):
        return lax.div(q, 4) * 2 + lax.rem(q, 2) + self.PL // 2 * lax.rem(lax.div(q, 2) + wave, 2)

    def plane_peer(self, q, i):
        return lax.rem(q + 1 + i, self.PL)

    def far_first(self, me, i):
        half = self.NZ // 2
        return (me + half + jnp.where(i % 2 == 1, (i + 1) // 2, self.NZ - i // 2)) % self.NZ

    def rank_of(self, e):
        z, xl = e // XL, e % XL
        return jnp.where(xl == z % 2, z, self.NZ + z)

    def owner(self, r):
        z = r % self.NZ
        return z * XL + (r + r // self.NZ) % 2


def kernel(pn, hid_hbm, w_hbm, bias_hbm, tgt_hbm, area_hbm, var_hbm, gp_hbm, f_hbm, x_ref,
           gp_ref, hid, w, bias, target, area, var, tgt, scl, varb, bcol, tmp, rem, S, R, G, B, pv, acc,
           xs, X, zx, PP, Q, zs, zr, U, F,
           in_sem, s_send, s_recv, g_send, b_recv, p_send, q_recv, z_send, z_recv, u_send, f_recv,
           out_sem, x_send, x_recv, zx_send, zx_recv):
    E, NG, NZ, VG, REM, NT, HC = pn.E, pn.NG, pn.NZ, pn.VG, pn.REM, pn.NT, pn.HC
    V, FULL, T, TAIL, NPL = pn.V, pn.FULL, pn.T, pn.TAIL, pn.PL
    NW = len(pn.WAVES)
    e = lax.axis_index("ens")
    g = lax.axis_index("grid")
    myz, myx = e // XL, e % XL
    r = pn.rank_of(e)
    q = g * XL + myx

    def plane(k):
        return {"ens": myz * XL + lax.rem(k, XL), "grid": lax.div(k, XL)}

    def column(k):
        return {"ens": k * XL + myx}

    def landed(ref, sem):
        pltpu.make_async_copy(ref, ref, sem).wait()

    def send(src, dst, send_sem, recv_sem, where):
        pltpu.make_async_remote_copy(
            src_ref=src, dst_ref=dst, send_sem=send_sem, recv_sem=recv_sem, device_id=where, device_id_type=MESH).start()

    barrier = pltpu.get_barrier_semaphore()

    @pl.loop(0, NZ)
    def _(i):
        z = pn.far_first(myz, i)
        for xl in range(XL):
            @pl.when(z * XL + xl != e)
            def _():
                pl.semaphore_signal(barrier, inc=1, device_id={"ens": z * XL + xl}, device_id_type=MESH)

    ins = [(w_hbm, w), (bias_hbm, bias), (tgt_hbm, target), (area_hbm, area), (var_hbm, var)]
    in_copies = [pltpu.make_async_copy(a, b, in_sem.at[i]) for i, (a, b) in enumerate(ins)]
    hid_copies = [
        pltpu.make_async_copy(hid_hbm.at[pl.ds(t * 128, 128)], hid.at[pl.ds(t * 128, 128)], in_sem.at[len(ins) + t])
        for t in range(NT)
    ]
    in_copies[0].start()
    in_copies[1].start()
    for c in hid_copies:
        c.start()
    for c in in_copies[2:]:
        c.start()

    @pl.loop(0, NPL - 1)
    def _(i):
        pl.semaphore_signal(barrier, inc=1, device_id=plane(pn.plane_peer(q, i)), device_id_type=MESH)

    in_copies[0].wait()
    in_copies[1].wait()
    varb[...] = jnp.zeros_like(varb)
    varb[:, 0:V] = jnp.broadcast_to(bias[...], (128, V))
    biasb = varb[...].T[0:V]
    rem[...] = jnp.zeros_like(rem)
    for t in range(NT):
        hid_copies[t].wait()
        raw = lax.dot_general(w[...], hid[t * 128:(t + 1) * 128], (((1,), (1,)), ((), ())), preferred_element_type=F32)
        pred = raw + biasb
        for vg in range(VG):
            S[vg * NT + t] = pred[16 * vg:16 * vg + 16].astype(BF16)
        rem[REM * t:REM * t + REM] = pred[16 * VG:V]
    for i in range(pn.RT):
        S[FULL + i] = rem[16 * i:16 * i + 16].astype(BF16)

    pl.semaphore_wait(barrier, E - 1 + NPL - 1)

    def send_tile(slot, j, rank):
        own = pn.owner(rank)

        @pl.when(own == e)
        def _():
            pltpu.make_async_copy(S.at[j], R.at[slot, e], s_recv.at[slot]).start()

        @pl.when(own != e)
        def _():
            send(S.at[j], R.at[slot, e], s_send.at[slot], s_recv.at[slot], {"ens": own})

    for wave in range(NW):
        lo, hi = pn.tiles(wave)

        @pl.loop(0, NZ)
        def _(i):
            z = pn.far_first(myz, i)
            for part in range(XL):
                if max(lo, part * NZ) < min(hi, part * NZ + NZ):
                    rank = z + part * NZ

                    @pl.when(jnp.logical_and(rank >= lo, rank < hi))
                    def _():
                        send_tile(0, rank, rank)

    @pl.loop(0, TAIL)
    def _(i):
        send_tile(1, E + i, i * pn.STEP)

    for c in in_copies[2:]:
        c.wait()
    varb[:, 0:V] = jnp.broadcast_to(var[...], (128, V))
    varb[...] = varb[...].T
    bcol[...] = jnp.zeros_like(bcol)

    tail_i = r // pn.STEP
    has_tail = jnp.logical_and(r % pn.STEP == 0, tail_i < TAIL)

    def prepare(slot, j):
        @pl.when(j < FULL)
        def _():
            vrow = pl.multiple_of((j // NT) * 16, 16)
            col = pl.multiple_of((j % NT) * 128, 128)
            tgt[slot] = target[pl.ds(vrow, 16), pl.ds(col, 128)]
            scl[slot] = varb[pl.ds(vrow, 16)] * area[pl.ds(j % NT, 1)]

        for i in range(pn.RT):
            @pl.when(j == FULL + i)
            def _():
                tgt[slot] = jnp.zeros((16, 128), F32)
                scl[slot] = jnp.zeros((16, 128), F32)
                for k in range(pn.FOLD):
                    t = i * pn.FOLD + k
                    if t < NT:
                        cols = slice(128 * t, 128 * t + 128)
                        tgt[slot, REM * k:REM * k + REM] = target[16 * VG:V, cols]
                        scl[slot, REM * k:REM * k + REM] = varb[16 * VG:V] * area[t:t + 1]

    prepare(0, r)

    @pl.when(has_tail)
    def _():
        prepare(1, E + tail_i)

    members = E
    eps = (1.0 - alpha_fair) / members
    pair_coef = (1.0 - eps) / (members - 1)
    c2 = smooth * smooth
    BM = E // 2

    def blocks(h, i, j, total, diag):
        rows = pl.ds(h * 8, 8)
        a = [pv[i * BM + k, rows] for k in range(BM)]
        b = a if diag else [pv[j * BM + k, rows] for k in range(BM)]
        sa = [acc[i * BM + k, rows] for k in range(BM)]
        sb = sa if diag else [acc[j * BM + k, rows] for k in range(BM)]
        for m in range(BM):
            for k in range(m + 1 if diag else 0, BM):
                d = a[m] - b[k]
                qq = d * d + c2
                rs = lax.rsqrt(qq)
                s = d * rs
                total = total + qq * rs
                sa[m] = sa[m] + s
                sb[k] = sb[k] - s
        for k in range(BM):
            acc[i * BM + k, rows] = sa[k]
            if not diag:
                acc[j * BM + k, rows] = sb[k]
        return total

    def process(slot, j):
        landed(R.at[slot], s_recv.at[slot])
        for m in range(E):
            pv[m] = R[slot, m].astype(F32)
            acc[m] = jnp.zeros((16, 128), F32)

        @pl.loop(0, 2)
        def _(h):
            total = blocks(h, 0, 0, jnp.zeros((8, 128), F32), True)
            total = blocks(h, 1, 1, total, True)
            tmp[pl.ds(h * 8, 8)] = blocks(h, 0, 1, total, False)
        tg, sc = tgt[slot], scl[slot]
        wave = pn.wave_of(j)

        def finish(i, carry):
            bsum, absum = carry
            z = pn.far_first(myz, i)
            for xl in range(XL):
                m = z * XL + xl
                d = pv[m] - tg
                qq = d * d + c2
                rs = lax.rsqrt(qq)
                gb = (sc * (d * rs - pair_coef * acc[m])).astype(BF16)
                G[slot, m] = gb
                bsum, absum = bsum + gb.astype(F32), absum + qq * rs

                @pl.when(m == e)
                def _():
                    pltpu.make_async_copy(G.at[slot, m], B.at[j], b_recv.at[wave]).start()

                @pl.when(m != e)
                def _():
                    send(G.at[slot, m], B.at[j], g_send.at[slot], b_recv.at[wave], {"ens": m})
            return bsum, absum
        zero = jnp.zeros((16, 128), F32)
        bsum, absum = lax.fori_loop(0, NZ, finish, (zero, zero))

        npair = members * (members - 1) // 2
        crps = (absum - members * smooth) / members - 2.0 * (pair_coef / (2.0 * members)) * (tmp[...] - npair * smooth)
        lossb = jnp.broadcast_to(jnp.sum(sc * crps, axis=(0, 1), keepdims=True), (8, 128))
        bcol[V + 4:V + 12] = bcol[V + 4:V + 12] + lossb
        bb = jnp.broadcast_to(jnp.sum(bsum, axis=1, keepdims=True), (16, 128))

        @pl.when(j < FULL)
        def _():
            rows = pl.ds(pl.multiple_of((j // NT) * 16, 16), 16)
            bcol[rows] = bcol[rows] + bb

        @pl.when(j >= FULL)
        def _():
            tmp[...] = bb
            fold = tmp[0:REM]
            for k in range(1, pn.FOLD):
                fold = fold + tmp[REM * k:REM * k + REM]
            bcol[16 * VG:V] = bcol[16 * VG:V] + fold

    @pl.loop(0, 2)
    def _(slot):
        @pl.when(jnp.logical_or(slot == 0, has_tail))
        def _():
            process(slot, jnp.where(slot == 0, r, E + tail_i))

    xs[...] = bcol[...].T[0:1]
    X[q] = xs[...]

    @pl.loop(0, NPL - 1)
    def _(i):
        send(xs, X.at[q], x_send, x_recv, plane(pn.plane_peer(q, i)))

    def home(wave):
        lo, hi = pn.tiles(wave)
        a, b = pn.WAVES[wave]
        last = b == VG
        landed(B.at[pl.ds(lo, hi - lo)], b_recv.at[wave])
        for t in range(NT):
            for vg in range(a, b):
                gp_ref[16 * vg:16 * vg + 16, 128 * t:128 * t + 128] = B[vg * NT + t]
        if last:
            for i in range(pn.RT):
                rem[16 * i:16 * i + 16] = B[FULL + i].astype(F32)
            for t in range(NT):
                gp_ref[16 * VG:V, 128 * t:128 * t + 128] = rem[REM * t:REM * t + REM].astype(BF16)
        rows = slice(16 * a, V if last else 16 * b)
        CW = 256
        n0 = pn.GW0[wave]
        for cc in range(pn.H // CW):
            part = lax.dot_general(
                gp_ref[rows], hid[:, cc * CW:(cc + 1) * CW], (((1,), (0,)), ((), ())), preferred_element_type=F32)
            for c2_ in range(CW // 128):
                c = cc * (CW // 128) + c2_
                cols = slice(128 * c2_, 128 * c2_ + 128)
                for vg in range(b - a):
                    PP[n0 + c * (b - a) + vg] = part[16 * vg:16 * vg + 16, cols].astype(BF16)
                if last:
                    rem[REM * c:REM * c + REM] = part[16 * (b - a):, cols]
        if last:
            for i in range(pn.RW):
                PP[n0 + HC * (b - a) + i] = rem[16 * i:16 * i + 16].astype(BF16)

        @pl.loop(0, NPL)
        def _(i):
            k = lax.rem(q + NPL // 2 + i, NPL)
            n = pn.owned(k, wave)

            @pl.when(jnp.logical_and(n < pn.GWT[wave], k == q))
            def _():
                pltpu.make_async_copy(PP.at[n0 + n], Q.at[wave, q], q_recv.at[wave]).start()

            @pl.when(jnp.logical_and(n < pn.GWT[wave], k != q))
            def _():
                send(PP.at[n0 + n], Q.at[wave, q], p_send.at[wave], q_recv.at[wave], plane(k))

    for wave in range(NW):
        home(wave)
    out_copies = [pltpu.make_async_copy(gp_ref, gp_hbm, out_sem.at[0])]
    out_copies[0].start()

    landed(X.at[pl.ds(0, NPL - 1)], x_recv)
    zx[myz] = lax.fori_loop(1, NPL, lambda i, s: s + X[i], X[0])

    @pl.loop(0, NZ - 1)
    def _(i):
        send(zx.at[myz], zx.at[myz], zx_send, zx_recv, column(pn.far_first(myz, i)))

    points = pn.G * NG
    mine = [pn.owned(q, wave) for wave in range(NW)]

    for wave in range(NW):
        @pl.when(mine[wave] < pn.GWT[wave])
        def _():
            landed(Q.at[wave], q_recv.at[wave])
            total = Q[wave, 0].astype(F32)
            for i in range(1, NPL):
                total = total + Q[wave, i].astype(F32)
            zs[wave] = total.astype(BF16)
            zr[wave, myz] = total.astype(BF16)

            @pl.loop(0, NZ - 1)
            def _(i):
                send(zs.at[wave], zr.at[wave, myz], z_send.at[wave], z_recv.at[wave], column(pn.far_first(myz, i)))

    for wave in range(NW):
        @pl.when(mine[wave] < pn.GWT[wave])
        def _():
            landed(zr.at[wave, pl.ds(0, NZ - 1)], z_recv.at[wave])
            total = zr[wave, 0].astype(F32)
            for i in range(1, NZ):
                total = total + zr[wave, i].astype(F32)
            U[wave] = (total * (1.0 / points)).astype(BF16)
            dst = F.at[pn.GW0[wave] + mine[wave]]
            pltpu.make_async_copy(U.at[wave], dst, f_recv.at[wave]).start()

            @pl.loop(0, NPL)
            def _(i):
                k = lax.rem(q + NPL // 2 + i, NPL)

                @pl.when(k != q)
                def _():
                    send(U.at[wave], dst, u_send.at[wave], f_recv.at[wave], plane(k))

    landed(zx.at[pl.ds(0, NZ - 1)], zx_recv)
    x_ref[...] = lax.fori_loop(0, NZ, lambda i, s: s + zx[i], jnp.zeros((1, 128), F32)) * (1.0 / points)

    landed(S.at[pl.ds(0, E - 1)], s_send.at[0])
    landed(G.at[0, pl.ds(0, E - 1)], g_send.at[0])
    landed(X.at[pl.ds(0, NPL - 1)], x_send)
    landed(zx.at[pl.ds(0, NZ - 1)], zx_send)

    @pl.when(has_tail)
    def _():
        landed(S.at[pl.ds(0, TAIL - 1)], s_send.at[1])
        landed(G.at[1, pl.ds(0, E - 1)], g_send.at[1])

    @pl.when(jnp.logical_not(has_tail))
    def _():
        landed(S.at[pl.ds(0, TAIL)], s_send.at[1])

    for wave in range(NW):
        n = pn.GWT[wave]

        @pl.when(mine[wave] < n)
        def _():
            landed(PP.at[pl.ds(0, n - 1)], p_send.at[wave])
            landed(zr.at[wave, pl.ds(0, NZ - 1)], z_send.at[wave])
            landed(Q.at[wave, pl.ds(0, NPL - 1)], u_send.at[wave])

        @pl.when(mine[wave] >= n)
        def _():
            landed(PP.at[pl.ds(0, n)], p_send.at[wave])

    for wave in range(NW):
        n0, n = pn.GW0[wave], pn.GWT[wave]
        landed(F.at[pl.ds(n0, n)], f_recv.at[wave])
        out_copies.append(pltpu.make_async_copy(F.at[pl.ds(n0, n)], f_hbm.at[pl.ds(n0, n)], out_sem.at[1 + wave]))
        out_copies[-1].start()
    for c in out_copies:
        c.wait()


def finish_kernel(pn, gp, w, f, x, loss_ref, gh_hbm, gw_hbm, gb_ref, gw, gh, rem, sems):
    V, VG, REM, HC = pn.V, pn.VG, pn.REM, pn.HC
    for wave, (a, b) in enumerate(pn.WAVES):
        for c in range(HC):
            for vg in range(a, b):
                gw[16 * vg:16 * vg + 16, 128 * c:128 * c + 128] = f[pn.GW0[wave] + c * (b - a) + vg - a].astype(F32)
    for i in range(pn.RW):
        rem[16 * i:16 * i + 16] = f[pn.GW0[-1] + pn.GWT[-1] - pn.RW + i].astype(F32)
    for c in range(HC):
        gw[16 * VG:V, 128 * c:128 * c + 128] = rem[REM * c:REM * c + REM]
    copies = [pltpu.make_async_copy(gw, gw_hbm, sems.at[0])]
    copies[0].start()
    for t in range(pn.NT):
        rows = slice(128 * t, 128 * t + 128)
        gh[rows] = lax.dot_general(
            gp[:, rows], w[...], (((0,), (0,)), ((), ())), preferred_element_type=F32).astype(BF16)
        out = pltpu.make_async_copy(gh.at[pl.ds(128 * t, 128)], gh_hbm.at[pl.ds(128 * t, 128)], sems.at[1 + t])
        out.start()
        copies.append(out)
    gb_ref[...] = x[0:1, 0:V]
    loss_ref[...] = x[0:1, V + 4:V + 5] * (1.0 / V)
    for out in copies:
        out.wait()


def body(mesh_shape, hidden, weight, bias, target, area_weight, var_weight):
    rows = hidden[0]
    V, H = weight.shape
    G = rows.shape[0]
    pn = Plan(mesh_shape, V, H, G)
    E, NZ = pn.E, pn.NZ
    NW = len(pn.WAVES)
    tile = (16, 128)
    NF = sum(pn.GWT)
    dma = pltpu.SemaphoreType.DMA
    vmem = pl.BlockSpec(memory_space=pltpu.VMEM)
    anywhere = pl.BlockSpec(memory_space=pl.ANY)
    gp, f, x = pl.pallas_call(
        functools.partial(kernel, pn),
        out_shape=(
            jax.ShapeDtypeStruct((V, G), BF16),
            jax.ShapeDtypeStruct((NF,) + tile, BF16),
            jax.ShapeDtypeStruct((1, 128), F32),
        ),
        in_specs=[anywhere] * 6,
        out_specs=(anywhere, anywhere, vmem),
        scratch_shapes=[
            pltpu.VMEM((V, G), BF16),
            pltpu.VMEM((G, H), BF16),
            pltpu.VMEM((V, H), BF16),
            pltpu.VMEM((1, V), F32),
            pltpu.VMEM((V, G), F32),
            pltpu.VMEM((pn.NT, 128), F32),
            pltpu.VMEM((1, V), F32),
            pltpu.VMEM((2,) + tile, F32),
            pltpu.VMEM((2,) + tile, F32),
            pltpu.VMEM((128, 128), F32),
            pltpu.VMEM((128, 128), F32),
            pltpu.VMEM(tile, F32),
            pltpu.VMEM((32, 128), F32),
            pltpu.VMEM((pn.T,) + tile, BF16),
            pltpu.VMEM((2, E) + tile, BF16),
            pltpu.VMEM((2, E) + tile, BF16),
            pltpu.VMEM((pn.T,) + tile, BF16),
            pltpu.VMEM((E,) + tile, F32),
            pltpu.VMEM((E,) + tile, F32),
            pltpu.VMEM((1, 128), F32),
            pltpu.VMEM((pn.PL, 1, 128), F32),
            pltpu.VMEM((NZ, 1, 128), F32),
            pltpu.VMEM((NF,) + tile, BF16),
            pltpu.VMEM((NW, pn.PL) + tile, BF16),
            pltpu.VMEM((NW,) + tile, BF16),
            pltpu.VMEM((NW, NZ) + tile, BF16),
            pltpu.VMEM((NW,) + tile, BF16),
            pltpu.VMEM((NF,) + tile, BF16),
            dma((5 + pn.NT,)),
            dma((2,)),
            dma((2,)),
            dma((2,)),
            dma((NW,)),
            dma((NW,)),
            dma((NW,)),
            dma((NW,)),
            dma((NW,)),
            dma((NW,)),
            dma((NW,)),
            dma((1 + NW,)),
            dma, dma, dma, dma,
        ],
        compiler_params=pltpu.CompilerParams(
            collective_id=0, has_side_effects=True, vmem_limit_bytes=60 * 1024 * 1024
        ),
        cost_estimate=pl.CostEstimate(flops=4 * V * G * H, bytes_accessed=2 * G * H, transcendentals=V * G * 16),
    )(rows, weight, bias[None], target, area_weight.reshape(-1, 128), var_weight[None])
    loss, gh, gw, gb = pl.pallas_call(
        functools.partial(finish_kernel, pn),
        out_shape=(
            jax.ShapeDtypeStruct((1, 1), F32),
            jax.ShapeDtypeStruct((G, H), BF16),
            jax.ShapeDtypeStruct((V, H), F32),
            jax.ShapeDtypeStruct((1, V), F32),
        ),
        in_specs=[vmem] * 4,
        out_specs=(vmem, anywhere, anywhere, vmem),
        scratch_shapes=[
            pltpu.VMEM((V, H), F32),
            pltpu.VMEM((G, H), BF16),
            pltpu.VMEM((32, 128), F32),
            dma((1 + pn.NT,)),
        ],
        compiler_params=pltpu.CompilerParams(vmem_limit_bytes=60 * 1024 * 1024),
        cost_estimate=pl.CostEstimate(flops=2 * V * G * H, bytes_accessed=2 * G * H, transcendentals=0),
    )(gp, weight, f, x)
    return (loss[0, 0], gh[None], gw, gb[0])


def solution(mesh):
    return jax.shard_map(
        functools.partial(body, dict(mesh.shape)),
        mesh=mesh,
        in_specs=(P("ens", "grid", None), P(), P(), P(None, "grid"), P("grid"), P()),
        out_specs=(P(), P("ens", "grid", None), P(), P()),
        check_vma=False,
    )
```

```python
import functools

import jax
import jax.numpy as jnp
from jax import lax
from jax.experimental import pallas as pl
from jax.experimental.pallas import tpu as pltpu
from jax.sharding import PartitionSpec as P

alpha_fair = 0.95
smooth = 0.3
MESH = pl.DeviceIdType.MESH
F32 = jnp.float32
BF16 = jnp.bfloat16
XL = 2


class Plan:
    def __init__(self, mesh_shape, V, H, G):
        self.E, self.NG = mesh_shape["ens"], mesh_shape["grid"]
        self.V, self.H, self.G = V, H, G
        self.NZ = self.E // XL
        self.VG, self.REM = V // 16, V % 16
        self.NT, self.HC = G // 128, H // 128
        self.FOLD = 16 // self.REM
        self.RT = -(-self.NT // self.FOLD)
        self.FULL = self.VG * self.NT
        self.T = self.FULL + self.RT
        self.TAIL = self.T - self.E
        self.STEP = max(1, self.NZ // max(1, self.TAIL))
        self.PL = XL * self.NG
        nw = min(3, self.VG)
        cuts = [self.VG * i // nw for i in range(nw + 1)]
        self.WAVES = tuple(zip(cuts[:-1], cuts[1:]))
        self.RW = -(-(self.REM * self.HC) // 16)
        self.GWT = tuple((b - a) * self.HC + (self.RW if b == self.VG else 0) for a, b in self.WAVES)
        self.GW0 = tuple(sum(self.GWT[:i]) for i in range(len(self.GWT)))

    def tiles(self, wave):
        a, b = self.WAVES[wave]
        return a * self.NT, self.T if b == self.VG else b * self.NT

    def wave_of(self, j):
        wave = 0
        for k in range(1, len(self.WAVES)):
            wave = wave + jnp.where(j >= self.tiles(k)[0], 1, 0)
        return wave

    def owned(self, q, wave):
        return lax.div(q, 4) * 2 + lax.rem(q, 2) + self.PL // 2 * lax.rem(lax.div(q, 2) + wave, 2)

    def plane_peer(self, q, i):
        return lax.rem(q + 1 + i, self.PL)

    def far_first(self, me, i):
        half = self.NZ // 2
        return (me + half + jnp.where(i % 2 == 1, (i + 1) // 2, self.NZ - i // 2)) % self.NZ

    def rank_of(self, e):
        z, xl = e // XL, e % XL
        return jnp.where(xl == z % 2, z, self.NZ + z)

    def owner(self, r):
        z = r % self.NZ
        return z * XL + (r + r // self.NZ) % 2


def kernel(pn, hid_hbm, w_hbm, bias_hbm, tgt_hbm, area_hbm, var_hbm, gp_hbm, f_hbm, x_ref,
           gp_ref, hid, w, bias, target, area, var, tgt, scl, varb, bcol, tmp, rem, S, R, G, B, pv, acc,
           xs, X, zx, PP, Q, zs, zr, U, F,
           in_sem, s_send, s_recv, g_send, b_recv, p_send, q_recv, z_send, z_recv, u_send, f_recv,
           out_sem, x_send, x_recv, zx_send, zx_recv):
    E, NG, NZ, VG, REM, NT, HC = pn.E, pn.NG, pn.NZ, pn.VG, pn.REM, pn.NT, pn.HC
    V, FULL, T, TAIL, NPL = pn.V, pn.FULL, pn.T, pn.TAIL, pn.PL
    NW = len(pn.WAVES)
    e = lax.axis_index("ens")
    g = lax.axis_index("grid")
    myz, myx = e // XL, e % XL
    r = pn.rank_of(e)
    q = g * XL + myx

    def plane(k):
        return {"ens": myz * XL + lax.rem(k, XL), "grid": lax.div(k, XL)}

    def column(k):
        return {"ens": k * XL + myx}

    def landed(ref, sem):
        pltpu.make_async_copy(ref, ref, sem).wait()

    def send(src, dst, send_sem, recv_sem, where):
        pltpu.make_async_remote_copy(
            src_ref=src, dst_ref=dst, send_sem=send_sem, recv_sem=recv_sem, device_id=where, device_id_type=MESH).start()

    barrier = pltpu.get_barrier_semaphore()

    @pl.loop(0, NZ)
    def _(i):
        z = pn.far_first(myz, i)
        for xl in range(XL):
            @pl.when(z * XL + xl != e)
            def _():
                pl.semaphore_signal(barrier, inc=1, device_id={"ens": z * XL + xl}, device_id_type=MESH)

    ins = [(w_hbm, w), (bias_hbm, bias), (tgt_hbm, target), (area_hbm, area), (var_hbm, var)]
    in_copies = [pltpu.make_async_copy(a, b, in_sem.at[i]) for i, (a, b) in enumerate(ins)]
    hid_copies = [
        pltpu.make_async_copy(hid_hbm.at[pl.ds(t * 128, 128)], hid.at[pl.ds(t * 128, 128)], in_sem.at[len(ins) + t])
        for t in range(NT)
    ]
    in_copies[0].start()
    in_copies[1].start()
    for c in hid_copies:
        c.start()
    for c in in_copies[2:]:
        c.start()

    @pl.loop(0, NPL - 1)
    def _(i):
        pl.semaphore_signal(barrier, inc=1, device_id=plane(pn.plane_peer(q, i)), device_id_type=MESH)

    in_copies[0].wait()
    in_copies[1].wait()
    varb[...] = jnp.zeros_like(varb)
    varb[:, 0:V] = jnp.broadcast_to(bias[...], (128, V))
    biasb = varb[...].T[0:V]
    rem[...] = jnp.zeros_like(rem)
    for t in range(NT):
        hid_copies[t].wait()
        raw = lax.dot_general(w[...], hid[t * 128:(t + 1) * 128], (((1,), (1,)), ((), ())), preferred_element_type=F32)
        pred = raw + biasb
        for vg in range(VG):
            S[vg * NT + t] = pred[16 * vg:16 * vg + 16].astype(BF16)
        rem[REM * t:REM * t + REM] = pred[16 * VG:V]
    for i in range(pn.RT):
        S[FULL + i] = rem[16 * i:16 * i + 16].astype(BF16)

    pl.semaphore_wait(barrier, E - 1 + NPL - 1)

    def send_tile(slot, j, rank):
        own = pn.owner(rank)

        @pl.when(own == e)
        def _():
            pltpu.make_async_copy(S.at[j], R.at[slot, e], s_recv.at[slot]).start()

        @pl.when(own != e)
        def _():
            send(S.at[j], R.at[slot, e], s_send.at[slot], s_recv.at[slot], {"ens": own})

    for wave in range(NW):
        lo, hi = pn.tiles(wave)

        @pl.loop(0, NZ)
        def _(i):
            z = pn.far_first(myz, i)
            for part in range(XL):
                if max(lo, part * NZ) < min(hi, part * NZ + NZ):
                    rank = z + part * NZ

                    @pl.when(jnp.logical_and(rank >= lo, rank < hi))
                    def _():
                        send_tile(0, rank, rank)

    @pl.loop(0, TAIL)
    def _(i):
        send_tile(1, E + i, i * pn.STEP)

    for c in in_copies[2:]:
        c.wait()
    varb[:, 0:V] = jnp.broadcast_to(var[...], (128, V))
    varb[...] = varb[...].T
    bcol[...] = jnp.zeros_like(bcol)

    tail_i = r // pn.STEP
    has_tail = jnp.logical_and(r % pn.STEP == 0, tail_i < TAIL)

    def prepare(slot, j):
        @pl.when(j < FULL)
        def _():
            vrow = pl.multiple_of((j // NT) * 16, 16)
            col = pl.multiple_of((j % NT) * 128, 128)
            tgt[slot] = target[pl.ds(vrow, 16), pl.ds(col, 128)]
            scl[slot] = varb[pl.ds(vrow, 16)] * area[pl.ds(j % NT, 1)]

        for i in range(pn.RT):
            @pl.when(j == FULL + i)
            def _():
                tgt[slot] = jnp.zeros((16, 128), F32)
                scl[slot] = jnp.zeros((16, 128), F32)
                for k in range(pn.FOLD):
                    t = i * pn.FOLD + k
                    if t < NT:
                        cols = slice(128 * t, 128 * t + 128)
                        tgt[slot, REM * k:REM * k + REM] = target[16 * VG:V, cols]
                        scl[slot, REM * k:REM * k + REM] = varb[16 * VG:V] * area[t:t + 1]

    prepare(0, r)

    @pl.when(has_tail)
    def _():
        prepare(1, E + tail_i)

    members = E
    eps = (1.0 - alpha_fair) / members
    pair_coef = (1.0 - eps) / (members - 1)
    c2 = smooth * smooth
    BM = E // 2

    def blocks(h, i, j, total, diag):
        rows = pl.ds(h * 8, 8)
        a = [pv[i * BM + k, rows] for k in range(BM)]
        b = a if diag else [pv[j * BM + k, rows] for k in range(BM)]
        sa = [acc[i * BM + k, rows] for k in range(BM)]
        sb = sa if diag else [acc[j * BM + k, rows] for k in range(BM)]
        for m in range(BM):
            for k in range(m + 1 if diag else 0, BM):
                d = a[m] - b[k]
                qq = d * d + c2
                rs = lax.rsqrt(qq)
                s = d * rs
                total = total + qq * rs
                sa[m] = sa[m] + s
                sb[k] = sb[k] - s
        for k in range(BM):
            acc[i * BM + k, rows] = sa[k]
            if not diag:
                acc[j * BM + k, rows] = sb[k]
        return total

    def process(slot, j):
        landed(R.at[slot], s_recv.at[slot])
        for m in range(E):
            pv[m] = R[slot, m].astype(F32)
            acc[m] = jnp.zeros((16, 128), F32)

        @pl.loop(0, 2)
        def _(h):
            total = blocks(h, 0, 0, jnp.zeros((8, 128), F32), True)
            total = blocks(h, 1, 1, total, True)
            tmp[pl.ds(h * 8, 8)] = blocks(h, 0, 1, total, False)
        tg, sc = tgt[slot], scl[slot]
        wave = pn.wave_of(j)

        def finish(i, carry):
            bsum, absum = carry
            z = pn.far_first(myz, i)
            for xl in range(XL):
                m = z * XL + xl
                d = pv[m] - tg
                qq = d * d + c2
                rs = lax.rsqrt(qq)
                gb = (sc * (d * rs - pair_coef * acc[m])).astype(BF16)
                G[slot, m] = gb
                bsum, absum = bsum + gb.astype(F32), absum + qq * rs

                @pl.when(m == e)
                def _():
                    pltpu.make_async_copy(G.at[slot, m], B.at[j], b_recv.at[wave]).start()

                @pl.when(m != e)
                def _():
                    send(G.at[slot, m], B.at[j], g_send.at[slot], b_recv.at[wave], {"ens": m})
            return bsum, absum
        zero = jnp.zeros((16, 128), F32)
        bsum, absum = lax.fori_loop(0, NZ, finish, (zero, zero))

        npair = members * (members - 1) // 2
        crps = (absum - members * smooth) / members - 2.0 * (pair_coef / (2.0 * members)) * (tmp[...] - npair * smooth)
        lossb = jnp.broadcast_to(jnp.sum(sc * crps, axis=(0, 1), keepdims=True), (8, 128))
        bcol[V + 4:V + 12] = bcol[V + 4:V + 12] + lossb
        bb = jnp.broadcast_to(jnp.sum(bsum, axis=1, keepdims=True), (16, 128))

        @pl.when(j < FULL)
        def _():
            rows = pl.ds(pl.multiple_of((j // NT) * 16, 16), 16)
            bcol[rows] = bcol[rows] + bb

        @pl.when(j >= FULL)
        def _():
            tmp[...] = bb
            fold = tmp[0:REM]
            for k in range(1, pn.FOLD):
                fold = fold + tmp[REM * k:REM * k + REM]
            bcol[16 * VG:V] = bcol[16 * VG:V] + fold

    @pl.loop(0, 2)
    def _(slot):
        @pl.when(jnp.logical_or(slot == 0, has_tail))
        def _():
            process(slot, jnp.where(slot == 0, r, E + tail_i))

    xs[...] = bcol[...].T[0:1]
    X[q] = xs[...]

    @pl.loop(0, NPL - 1)
    def _(i):
        send(xs, X.at[q], x_send, x_recv, plane(pn.plane_peer(q, i)))

    def home(wave):
        lo, hi = pn.tiles(wave)
        a, b = pn.WAVES[wave]
        last = b == VG
        landed(B.at[pl.ds(lo, hi - lo)], b_recv.at[wave])
        for t in range(NT):
            for vg in range(a, b):
                gp_ref[16 * vg:16 * vg + 16, 128 * t:128 * t + 128] = B[vg * NT + t]
        if last:
            for i in range(pn.RT):
                rem[16 * i:16 * i + 16] = B[FULL + i].astype(F32)
            for t in range(NT):
                gp_ref[16 * VG:V, 128 * t:128 * t + 128] = rem[REM * t:REM * t + REM].astype(BF16)
        rows = slice(16 * a, V if last else 16 * b)
        CW = 256
        n0 = pn.GW0[wave]
        for cc in range(pn.H // CW):
            part = lax.dot_general(
                gp_ref[rows], hid[:, cc * CW:(cc + 1) * CW], (((1,), (0,)), ((), ())), preferred_element_type=F32)
            for c2_ in range(CW // 128):
                c = cc * (CW // 128) + c2_
                cols = slice(128 * c2_, 128 * c2_ + 128)
                for vg in range(b - a):
                    PP[n0 + c * (b - a) + vg] = part[16 * vg:16 * vg + 16, cols].astype(BF16)
                if last:
                    rem[REM * c:REM * c + REM] = part[16 * (b - a):, cols]
        if last:
            for i in range(pn.RW):
                PP[n0 + HC * (b - a) + i] = rem[16 * i:16 * i + 16].astype(BF16)

        @pl.loop(0, NPL)
        def _(i):
            k = lax.rem(q + NPL // 2 + i, NPL)
            n = pn.owned(k, wave)

            @pl.when(jnp.logical_and(n < pn.GWT[wave], k == q))
            def _():
                pltpu.make_async_copy(PP.at[n0 + n], Q.at[wave, q], q_recv.at[wave]).start()

            @pl.when(jnp.logical_and(n < pn.GWT[wave], k != q))
            def _():
                send(PP.at[n0 + n], Q.at[wave, q], p_send.at[wave], q_recv.at[wave], plane(k))

    for wave in range(NW):
        home(wave)
    out_copies = [pltpu.make_async_copy(gp_ref, gp_hbm, out_sem.at[0])]
    out_copies[0].start()

    landed(X.at[pl.ds(0, NPL - 1)], x_recv)
    zx[myz] = lax.fori_loop(1, NPL, lambda i, s: s + X[i], X[0])

    @pl.loop(0, NZ - 1)
    def _(i):
        send(zx.at[myz], zx.at[myz], zx_send, zx_recv, column(pn.far_first(myz, i)))

    points = pn.G * NG
    mine = [pn.owned(q, wave) for wave in range(NW)]

    for wave in range(NW):
        @pl.when(mine[wave] < pn.GWT[wave])
        def _():
            landed(Q.at[wave], q_recv.at[wave])
            total = Q[wave, 0].astype(F32)
            for i in range(1, NPL):
                total = total + Q[wave, i].astype(F32)
            zs[wave] = total.astype(BF16)
            zr[wave, myz] = total.astype(BF16)

            @pl.loop(0, NZ - 1)
            def _(i):
                send(zs.at[wave], zr.at[wave, myz], z_send.at[wave], z_recv.at[wave], column(pn.far_first(myz, i)))

    for wave in range(NW):
        @pl.when(mine[wave] < pn.GWT[wave])
        def _():
            landed(zr.at[wave, pl.ds(0, NZ - 1)], z_recv.at[wave])
            total = zr[wave, 0].astype(F32)
            for i in range(1, NZ):
                total = total + zr[wave, i].astype(F32)
            U[wave] = (total * (1.0 / points)).astype(BF16)
            dst = F.at[pn.GW0[wave] + mine[wave]]
            pltpu.make_async_copy(U.at[wave], dst, f_recv.at[wave]).start()

            @pl.loop(0, NPL)
            def _(i):
                k = lax.rem(q + NPL // 2 + i, NPL)

                @pl.when(k != q)
                def _():
                    send(U.at[wave], dst, u_send.at[wave], f_recv.at[wave], plane(k))

    landed(zx.at[pl.ds(0, NZ - 1)], zx_recv)
    x_ref[...] = lax.fori_loop(0, NZ, lambda i, s: s + zx[i], jnp.zeros((1, 128), F32)) * (1.0 / points)

    landed(S.at[pl.ds(0, E - 1)], s_send.at[0])
    landed(G.at[0, pl.ds(0, E - 1)], g_send.at[0])
    landed(X.at[pl.ds(0, NPL - 1)], x_send)
    landed(zx.at[pl.ds(0, NZ - 1)], zx_send)

    @pl.when(has_tail)
    def _():
        landed(S.at[pl.ds(0, TAIL - 1)], s_send.at[1])
        landed(G.at[1, pl.ds(0, E - 1)], g_send.at[1])

    @pl.when(jnp.logical_not(has_tail))
    def _():
        landed(S.at[pl.ds(0, TAIL)], s_send.at[1])

    for wave in range(NW):
        n = pn.GWT[wave]

        @pl.when(mine[wave] < n)
        def _():
            landed(PP.at[pl.ds(0, n - 1)], p_send.at[wave])
            landed(zr.at[wave, pl.ds(0, NZ - 1)], z_send.at[wave])
            landed(Q.at[wave, pl.ds(0, NPL - 1)], u_send.at[wave])

        @pl.when(mine[wave] >= n)
        def _():
            landed(PP.at[pl.ds(0, n)], p_send.at[wave])

    for wave in range(NW):
        n0, n = pn.GW0[wave], pn.GWT[wave]
        landed(F.at[pl.ds(n0, n)], f_recv.at[wave])
        out_copies.append(pltpu.make_async_copy(F.at[pl.ds(n0, n)], f_hbm.at[pl.ds(n0, n)], out_sem.at[1 + wave]))
        out_copies[-1].start()
    for c in out_copies:
        c.wait()


def finish_kernel(pn, gp, w, f, x, loss_ref, gh_hbm, gw_hbm, gb_ref, gw, gh, rem, sems):
    V, VG, REM, HC = pn.V, pn.VG, pn.REM, pn.HC
    for wave, (a, b) in enumerate(pn.WAVES):
        for c in range(HC):
            for vg in range(a, b):
                gw[16 * vg:16 * vg + 16, 128 * c:128 * c + 128] = f[pn.GW0[wave] + c * (b - a) + vg - a].astype(F32)
    for i in range(pn.RW):
        rem[16 * i:16 * i + 16] = f[pn.GW0[-1] + pn.GWT[-1] - pn.RW + i].astype(F32)
    for c in range(HC):
        gw[16 * VG:V, 128 * c:128 * c + 128] = rem[REM * c:REM * c + REM]
    copies = [pltpu.make_async_copy(gw, gw_hbm, sems.at[0])]
    copies[0].start()
    for t in range(pn.NT):
        rows = slice(128 * t, 128 * t + 128)
        gh[rows] = lax.dot_general(
            gp[:, rows], w[...], (((0,), (0,)), ((), ())), preferred_element_type=F32).astype(BF16)
        out = pltpu.make_async_copy(gh.at[pl.ds(128 * t, 128)], gh_hbm.at[pl.ds(128 * t, 128)], sems.at[1 + t])
        out.start()
        copies.append(out)
    gb_ref[...] = x[0:1, 0:V]
    loss_ref[...] = x[0:1, V + 4:V + 5] * (1.0 / V)
    for out in copies:
        out.wait()


def body(mesh_shape, hidden, weight, bias, target, area_weight, var_weight):
    rows = hidden[0]
    V, H = weight.shape
    G = rows.shape[0]
    pn = Plan(mesh_shape, V, H, G)
    E, NZ = pn.E, pn.NZ
    NW = len(pn.WAVES)
    tile = (16, 128)
    NF = sum(pn.GWT)
    dma = pltpu.SemaphoreType.DMA
    vmem = pl.BlockSpec(memory_space=pltpu.VMEM)
    anywhere = pl.BlockSpec(memory_space=pl.ANY)
    gp, f, x = pl.pallas_call(
        functools.partial(kernel, pn),
        out_shape=(
            jax.ShapeDtypeStruct((V, G), BF16),
            jax.ShapeDtypeStruct((NF,) + tile, BF16),
            jax.ShapeDtypeStruct((1, 128), F32),
        ),
        in_specs=[anywhere] * 6,
        out_specs=(anywhere, anywhere, vmem),
        scratch_shapes=[
            pltpu.VMEM((V, G), BF16),
            pltpu.VMEM((G, H), BF16),
            pltpu.VMEM((V, H), BF16),
            pltpu.VMEM((1, V), F32),
            pltpu.VMEM((V, G), F32),
            pltpu.VMEM((pn.NT, 128), F32),
            pltpu.VMEM((1, V), F32),
            pltpu.VMEM((2,) + tile, F32),
            pltpu.VMEM((2,) + tile, F32),
            pltpu.VMEM((128, 128), F32),
            pltpu.VMEM((128, 128), F32),
            pltpu.VMEM(tile, F32),
            pltpu.VMEM((32, 128), F32),
            pltpu.VMEM((pn.T,) + tile, BF16),
            pltpu.VMEM((2, E) + tile, BF16),
            pltpu.VMEM((2, E) + tile, BF16),
            pltpu.VMEM((pn.T,) + tile, BF16),
            pltpu.VMEM((E,) + tile, F32),
            pltpu.VMEM((E,) + tile, F32),
            pltpu.VMEM((1, 128), F32),
            pltpu.VMEM((pn.PL, 1, 128), F32),
            pltpu.VMEM((NZ, 1, 128), F32),
            pltpu.VMEM((NF,) + tile, BF16),
            pltpu.VMEM((NW, pn.PL) + tile, BF16),
            pltpu.VMEM((NW,) + tile, BF16),
            pltpu.VMEM((NW, NZ) + tile, BF16),
            pltpu.VMEM((NW,) + tile, BF16),
            pltpu.VMEM((NF,) + tile, BF16),
            dma((5 + pn.NT,)),
            dma((2,)),
            dma((2,)),
            dma((2,)),
            dma((NW,)),
            dma((NW,)),
            dma((NW,)),
            dma((NW,)),
            dma((NW,)),
            dma((NW,)),
            dma((NW,)),
            dma((1 + NW,)),
            dma, dma, dma, dma,
        ],
        compiler_params=pltpu.CompilerParams(
            collective_id=0, has_side_effects=True, vmem_limit_bytes=60 * 1024 * 1024
        ),
        cost_estimate=pl.CostEstimate(flops=4 * V * G * H, bytes_accessed=2 * G * H, transcendentals=V * G * 16),
    )(rows, weight, bias[None], target, area_weight.reshape(-1, 128), var_weight[None])
    loss, gh, gw, gb = pl.pallas_call(
        functools.partial(finish_kernel, pn),
        out_shape=(
            jax.ShapeDtypeStruct((1, 1), F32),
            jax.ShapeDtypeStruct((G, H), BF16),
            jax.ShapeDtypeStruct((V, H), F32),
            jax.ShapeDtypeStruct((1, V), F32),
        ),
        in_specs=[vmem] * 4,
        out_specs=(vmem, anywhere, anywhere, vmem),
        scratch_shapes=[
            pltpu.VMEM((V, H), F32),
            pltpu.VMEM((G, H), BF16),
            pltpu.VMEM((32, 128), F32),
            dma((1 + pn.NT,)),
        ],
        compiler_params=pltpu.CompilerParams(vmem_limit_bytes=60 * 1024 * 1024),
        cost_estimate=pl.CostEstimate(flops=2 * V * G * H, bytes_accessed=2 * G * H, transcendentals=0),
    )(gp, weight, f, x)
    return (loss[0, 0], gh[None], gw, gb[0])


def solution(mesh):
    return jax.shard_map(
        functools.partial(body, dict(mesh.shape)),
        mesh=mesh,
        in_specs=(P("ens", "grid", None), P(), P(), P(None, "grid"), P("grid"), P()),
        out_specs=(P(), P("ens", "grid", None), P(), P()),
        check_vma=False,
    )
```
